128 devices in a mesh: agent: 16 (over x_hi, z, core), seq: 8 (over y, x_lo).
Axes of the slice: x: 4 (x_hi: 2, x_lo: 2; x = x_hi * 2 + x_lo), y: 4, z: 4, core: 2. Of those that a mesh axis runs over, the one named last changes fastest.
Arguments:
- queries: bfloat16 [16, 1024, 1024], P('agent', 'seq'), may hold values from -8 to 8
- key_codes: bfloat16 [16, 1024, 1024], P('agent', 'seq'), may hold values from -8 to 8
- key_exps: int32 [16, 8, 8], P('agent', 'seq'), may hold values from -1 to 1
- value_codes: bfloat16 [16, 1024, 1024], P('agent', 'seq'), may hold values from -6 to 6
- value_exps: int32 [16, 8, 8], P('agent', 'seq'), may hold values from -1 to 1
- d_out: bfloat16 [16, 1024, 2048], P('agent', 'seq'), may hold values from -6 to 6
- out_weight: float32 [16, 1024, 2048], P('agent', 'seq'), may hold values from -0.1875 to 0.1875
- prev_psi: float32 [16, 1024, 2048], P('agent', 'seq'), may hold values from -0.1875 to 0.1875
- mixing: int32 [16, 2], P('agent'), may hold values from 1 to 4, as said below
Outputs:
- d_queries: bfloat16 [16, 1024, 1024], P('agent', 'seq')
- d_keys: bfloat16 [16, 1024, 1024], P('agent', 'seq')
- d_values: bfloat16 [16, 1024, 1024], P('agent', 'seq')
- new_weight: float32 [16, 1024, 2048], P('agent', 'seq')
- new_psi: float32 [16, 1024, 2048], P('agent', 'seq')
The draws below stay inside these ranges and needn't reach their ends.
Inputs may be any that keep to these rules, and one draw needn't show every extreme that they name: mixing[a, 1] equals mixing[a + 1, 0] with agent indices modulo 16: one numerator for each edge of the loop, so that the mixing matrix is symmetric and doubly stochastic with an own weight of one half or more; in every draw some edge has the numerator 1 and some edge 4.
All inputs are finite; a program needn't handle non-finite values.
Results may differ from the reference program's by a relative error of at most 0.035.
Values may be sent and summed in bfloat16 or wider, within the bound.
A program may use at most 128 MiB of HBM per device.

```python
import jax
import jax.numpy as jnp
from jax import lax

D = 2048
HEADS = 8
HDIM = 128
SBLK = 128
TOK_DEV = 128
HD = 1024
TOKENS = 1024
AGENTS = 16
N_SEQ = 8


def draw_queries(key, part):
    key = jax.random.fold_in(key, 11)
    base = jnp.clip(jax.random.normal(key, (AGENTS, TOKENS, HEADS, HDIM), jnp.float32), -6.0, 6.0)
    return base.reshape(AGENTS, TOKENS, HEADS * HDIM).astype(jnp.bfloat16)


def draw_key_codes(key, part):
    key = jax.random.fold_in(key, 12)
    base = jnp.clip(jax.random.normal(key, (AGENTS, TOKENS, HEADS, HDIM), jnp.float32), -6.0, 6.0)
    return base.reshape(AGENTS, TOKENS, HEADS * HDIM).astype(jnp.bfloat16)


def draw_mixing(key, part):
    key = jax.random.fold_in(key, 13)
    subkeys = jax.random.split(key, 3)
    edges = jax.random.randint(subkeys[0], (AGENTS,), 1, 5)
    agent_ids = jnp.arange(AGENTS, dtype=jnp.int32)
    highest = jax.random.randint(subkeys[1], (), 0, AGENTS)
    lowest = (highest + jax.random.randint(subkeys[2], (), 1, AGENTS)) % AGENTS
    edges = jnp.where(agent_ids == highest, 4, jnp.where(agent_ids == lowest, 1, edges))
    return jnp.stack([edges, jnp.roll(edges, -1)], axis=1).astype(jnp.int32)


def touch_ends(result, rng, smallest, top_value):
    longest = result.shape.index(max(result.shape))
    spots = []
    for shift in (0, 1):
        where = [jax.random.randint(jax.random.fold_in(rng, axis), (), 0, length) for axis, length in enumerate(result.shape)]
        where[longest] = (where[longest] + shift) % result.shape[longest]
        spots.append(tuple(where))
    return result.at[spots[0]].set(smallest).at[spots[1]].set(top_value)


def level_of(key, shape, cuts, least, largest):
    level, own = 1.0, jax.random.fold_in(key, 6)
    for position, parts in cuts:
        draws = jnp.exp(jax.random.uniform(jax.random.fold_in(own, position), (parts,), jnp.float32, least / len(cuts), largest / len(cuts)))
        level = level * jnp.repeat(draws, shape[position] // parts).reshape([-1 if axis == position else 1 for axis in range(len(shape))])
    return level


def bell_draw(key, dims, spread, limit, cuts=(), held_as=jnp.bfloat16):
    drawn = jax.random.normal(key, dims, jnp.float32) * spread
    if len(cuts) > 0:
        drawn = level_of(key, dims, cuts, -0.22, 0.18) * drawn
    return jnp.clip(drawn, min=-limit, max=limit).astype(held_as)


def setup_inputs(seed: int = 0) -> dict:
    key_of = jax.random.split(jax.random.key(seed), 10)
    return {
        "queries": draw_queries(jax.random.fold_in(key_of[9], 71), 0),
        "key_codes": draw_key_codes(jax.random.fold_in(key_of[9], 71), 0),
        "key_exps": touch_ends(jax.random.randint(key_of[2], (AGENTS, TOKENS // SBLK, HEADS), -1, 2), jax.random.fold_in(key_of[2], 1), -1, 1).astype(jnp.int32),
        "value_codes": bell_draw(key_of[3], (AGENTS, TOKENS, HD), 1.0, 6.0, ((0, 16), (1, 8))),
        "value_exps": touch_ends(jax.random.randint(key_of[4], (AGENTS, TOKENS // SBLK, HEADS), -1, 2), jax.random.fold_in(key_of[4], 1), -1, 1).astype(jnp.int32),
        "d_out": bell_draw(key_of[5], (AGENTS, TOKENS, D), 1.0, 6.0, ((0, 16), (1, 8))),
        "out_weight": bell_draw(key_of[6], (AGENTS, HD, D), HD ** -0.5, 0.1875, ((0, 16), (1, 8)), jnp.float32),
        "prev_psi": bell_draw(key_of[7], (AGENTS, HD, D), HD ** -0.5, 0.1875, ((0, 16), (1, 8)), jnp.float32),
        "mixing": draw_mixing(jax.random.fold_in(key_of[9], 71), 0),
    }


def dequant(code, expo):
    factor = jnp.exp2(expo.astype(jnp.float32))
    blocks = code.astype(jnp.float32).reshape(expo.shape[0], SBLK, HEADS, HDIM) * factor[:, None, :, None]
    return blocks.reshape(code.shape).astype(jnp.bfloat16)


def head_probs(q_head, k_head, scale):
    scores = jnp.dot(q_head, k_head.T, preferred_element_type=jnp.float32) * scale
    top = jnp.max(scores, axis=-1, keepdims=True)
    lse = top + jnp.log(jnp.sum(jnp.exp(scores - top), axis=-1, keepdims=True))
    return jnp.exp(scores - lse)


def rounded(partial_value):
    return lax.optimization_barrier(partial_value.astype(jnp.bfloat16)).astype(jnp.float32)


def block_sum(left, right):
    total = jnp.zeros((left.shape[1], right.shape[1]), jnp.float32)
    for block in range(N_SEQ):
        rows = slice(block * TOK_DEV, (block + 1) * TOK_DEV)
        total = total + rounded(jnp.dot(left[rows].T, right[rows], preferred_element_type=jnp.float32))
    return total


def agent_grads(inputs):
    queries, key_codes, key_exps, value_codes, value_exps, d_out, weight = inputs
    keys = dequant(key_codes, key_exps)
    values = dequant(value_codes, value_exps)
    scale = HDIM ** -0.5
    outputs = []
    for head in range(HEADS):
        cols = slice(head * HDIM, (head + 1) * HDIM)
        prob = head_probs(queries[:, cols], keys[:, cols], scale)
        outputs.append(jnp.dot(prob.astype(jnp.bfloat16), values[:, cols], preferred_element_type=jnp.float32).astype(jnp.bfloat16))
    attn = jnp.concatenate(outputs, axis=1)
    weight_b = weight.astype(jnp.bfloat16)
    d_attn = jnp.dot(d_out, weight_b.T, preferred_element_type=jnp.float32).astype(jnp.bfloat16)
    grad_w = block_sum(attn, d_out)
    dq_list, dk_list, dv_list = [], [], []
    for head in range(HEADS):
        cols = slice(head * HDIM, (head + 1) * HDIM)
        prob = head_probs(queries[:, cols], keys[:, cols], scale)
        dprob = jnp.dot(d_attn[:, cols], values[:, cols].T, preferred_element_type=jnp.float32)
        row_dot = jnp.sum(d_attn[:, cols].astype(jnp.float32) * attn[:, cols].astype(jnp.float32), axis=-1, keepdims=True)
        dscore = (prob * (dprob - row_dot) * scale).astype(jnp.bfloat16)
        dq_list.append(jnp.dot(dscore, keys[:, cols], preferred_element_type=jnp.float32).astype(jnp.bfloat16))
        dk_list.append(block_sum(dscore, queries[:, cols]).astype(jnp.bfloat16))
        dv_list.append(block_sum(prob.astype(jnp.bfloat16), d_attn[:, cols]).astype(jnp.bfloat16))
    return (jnp.concatenate(dq_list, axis=1), jnp.concatenate(dk_list, axis=1), jnp.concatenate(dv_list, axis=1), grad_w)


def reference(queries, key_codes, key_exps, value_codes, value_exps, d_out, out_weight, prev_psi, mixing):
    d_queries, d_keys, d_values, grad_w = lax.map(agent_grads, (queries, key_codes, key_exps, value_codes, value_exps, d_out, out_weight))
    new_psi = out_weight - 0.02 * grad_w
    phi = new_psi + out_weight - prev_psi
    numer = mixing.astype(jnp.float32)
    before = numer[:, 0][:, None, None]
    after = numer[:, 1][:, None, None]
    own = 16.0 - before - after
    new_weight = (own * phi + before * jnp.roll(phi, 1, axis=0) + after * jnp.roll(phi, -1, axis=0)) * 0.0625
    return d_queries, d_keys, d_values, new_weight, new_psi
```

```python
import jax
import jax.numpy as jnp
from jax import lax
from jax.experimental import pallas as pl
from jax.experimental.pallas import tpu as pltpu
from jax.sharding import PartitionSpec as P

HEADS = 8
HDIM = 128
TOK = 128
N_SEQ = 8
N_AGENT = 16
TOKENS = N_SEQ * TOK
HD = HEADS * HDIM
D = 2048
PAIR = 2 * TOK
N_PAIR = TOKENS // PAIR
SCALE = HDIM ** (-0.5)
MESH = pl.DeviceIdType.MESH

A1, A2, B1, B2 = (0, 640), (640, 512), (1152, 384), (1536, 512)
PIECES = {"A1": A1, "A2": A2, "B1": B1, "B2": B2}


def _gather_messages():
    msgs = []
    for p in ("B1", "B2", "A1", "A2"):
        msgs.append(("P" + p, "dn", (-1, 0), p))
        msgs.append(("M" + p, "up", (1, 0), p))
        msgs.append(("X" + p, "xp", (0, 1), p))
    for p in ("A1", "A2"):
        msgs.append(("PX" + p, "dn", (-1, 1), p))
        msgs.append(("MX" + p, "up", (1, 1), p))
    msgs.append(("P2A1", "dn", (-2, 0), "A1"))
    msgs.append(("P2XA1", "dn", (-2, 1), "A1"))
    msgs.append(("P2B1", "dn", (-2, 0), "B1"))
    msgs.append(("M2A2", "up", (2, 0), "A2"))
    msgs.append(("M2XA2", "up", (2, 1), "A2"))
    msgs.append(("M2B2", "up", (2, 0), "B2"))
    for p in ("B1", "B2"):
        msgs.append(("XP" + p, "xp", (-1, 1), p))
        msgs.append(("XM" + p, "xp", (1, 1), p))
    msgs.append(("XP2B1", "xp", (-2, 1), "B1"))
    msgs.append(("XM2B2", "xp", (2, 1), "B2"))
    return msgs


MSGS = _gather_messages()
KIND = {m[0]: i for i, m in enumerate(MSGS)}
N_MSG = len(MSGS)


def nt(a, b):
    return lax.dot_general(a, b, (((1,), (1,)), ((), ())), preferred_element_type=jnp.float32)


def nn(a, b):
    return jnp.dot(a, b, preferred_element_type=jnp.float32)


def kernel(
    mix_ref, ke_ref, ve_ref, q_hbm, kc_hbm, vc_hbm, do_hbm, w_hbm, ps_hbm,
    dq_out, dk_out, dv_out, nw_out, np_out,
    kc_v, vc_v, k_st, v_st, qh, kh, vh, kt, vt, do_all, w_f, ps_f, w_t,
    pt, at, gw, dk_acc, dv_acc, dq_st, dk_st, dv_st, phi_b, halo,
    load_sem, own_sem, a2a_s, a2a_r, ag_s, ag_r, back_s, back_r, halo_s, halo_r,
):
    me = lax.axis_index("seq")
    agent = lax.axis_index("agent")
    y, x = me // 2, lax.rem(me, 2)

    def at_rel(dy, dx):
        return lax.rem(y + (dy + 8), 4) * 2 + lax.rem(x + dx, 2)

    def rows(block):
        return pl.ds(pl.multiple_of(block * TOK, TOK), TOK)

    def cols(block):
        return pl.ds(pl.multiple_of(block * HDIM, HDIM), HDIM)

    rels = [(dy, dx) for dy in range(4) for dx in range(2)]
    peers = rels[1:]

    loads = {}
    for i, (name, src, dst) in enumerate(
        (
            ("k", kc_hbm, kc_v),
            ("v", vc_hbm, vc_v),
            ("q", q_hbm.at[:, cols(me)], qh.at[rows(me), :]),
            ("w", w_hbm, w_f),
            ("d", do_hbm, do_all.at[rows(me), :]),
            ("p", ps_hbm, ps_f),
        )
    ):
        loads[name] = pltpu.make_async_copy(src, dst, load_sem.at[i])
        loads[name].start()

    barrier = pltpu.get_barrier_semaphore()
    for dy, dx in peers:
        pl.semaphore_signal(barrier, inc=1, device_id={"seq": at_rel(dy, dx)}, device_id_type=MESH)
    nxt, prv = lax.rem(agent + 1, N_AGENT), lax.rem(agent + N_AGENT - 1, N_AGENT)
    for other in (nxt, prv):
        pl.semaphore_signal(barrier, inc=1, device_id={"agent": other}, device_id_type=MESH)
    pl.semaphore_wait(barrier, len(peers) + 2)

    sent = []

    def push(src, dst, ssem, rsem, target):
        copy = pltpu.make_async_remote_copy(
            src_ref=src, dst_ref=dst, send_sem=ssem, recv_sem=rsem,
            device_id=target, device_id_type=MESH,
        )
        copy.start()
        sent.append(copy)

    def arrived(dst, rsem, ssem):
        pltpu.make_async_remote_copy(
            src_ref=dst, dst_ref=dst, send_sem=ssem, recv_sem=rsem,
            device_id={"seq": at_rel(0, 1)}, device_id_type=MESH,
        ).wait_recv()

    def a2a_send(j, src, dst):
        for r, (dy, dx) in enumerate(rels):
            if r:
                t = at_rel(dy, dx)
                push(src.at[:, cols(t)], dst.at[rows(me), :], a2a_s.at[j, r], a2a_r.at[j, r],
                     {"seq": t})

    def a2a_wait(j, dst):
        for r, (dy, dx) in enumerate(rels):
            if r:
                arrived(dst.at[rows(at_rel(-dy, dx)), :], a2a_r.at[j, r], a2a_s.at[j, r])

    def scaled(codes, expo, out):
        factor = jnp.exp2(expo[...].astype(jnp.float32))
        for h in range(HEADS):
            c = slice(h * HDIM, (h + 1) * HDIM)
            out[:, c] = (codes[:, c].astype(jnp.float32) * factor[0:1, h : h + 1]).astype(
                jnp.bfloat16
            )

    a2a_send(0, q_hbm, qh)
    loads["k"].wait()
    scaled(kc_v, ke_ref, k_st)
    a2a_send(1, k_st, kh)
    loads["v"].wait()
    scaled(vc_v, ve_ref, v_st)
    a2a_send(2, v_st, vh)

    step = {"xp": (0, 1), "up": (1, 0), "dn": (-1, 0)}
    back_to = {"xp": "xp", "up": "dn", "dn": "up"}

    def ag_send(name, own=False):
        kind = KIND[name]
        _, source, (dy, dx), piece = MSGS[kind]
        sy, sx = step[source]
        ty, tx = step[back_to[source]]
        block = at_rel(dy - sy, (dx + sx) % 2)
        first, width = PIECES[piece]
        here = do_all.at[rows(block), pl.ds(first, width)]
        src = do_hbm.at[:, pl.ds(first, width)] if own else here
        push(src, here, ag_s.at[kind], ag_r.at[kind], {"seq": at_rel(ty, tx)})

    def ag_wait(name):
        kind = KIND[name]
        _, _, (dy, dx), piece = MSGS[kind]
        first, width = PIECES[piece]
        arrived(do_all.at[rows(at_rel(dy, dx)), pl.ds(first, width)], ag_r.at[kind], ag_s.at[kind])

    for name in ("PB1", "MB2", "XA1", "PB2", "MB1", "XA2", "PA1", "MA2", "PA2", "MA1", "XB1", "XB2"):
        ag_send(name, own=True)

    own_k = pltpu.make_async_copy(k_st.at[:, cols(me)], kh.at[rows(me), :], own_sem.at[0])
    own_v = pltpu.make_async_copy(v_st.at[:, cols(me)], vh.at[rows(me), :], own_sem.at[1])
    own_k.start()
    own_v.start()

    loads["w"].wait()
    for c in range(0, D, 256):
        w_t[c : c + 256, :] = w_f[:, c : c + 256].T.astype(jnp.bfloat16)
    dk_acc[...] = jnp.zeros_like(dk_acc)
    dv_acc[...] = jnp.zeros_like(dv_acc)
    gw[...] = jnp.zeros_like(gw)

    def stage_b():
        ag_wait("PB1")
        ag_send("P2B1")
        ag_send("XPB1")
        ag_wait("MB2")
        ag_send("M2B2")
        ag_send("XMB2")
        ag_wait("PB2")
        ag_send("XPB2")
        ag_wait("MB1")
        ag_send("XMB1")

    def stage_x():
        ag_wait("XA1")
        ag_send("PXA1")
        ag_send("MXA1")
        ag_wait("XA2")
        ag_send("PXA2")
        ag_send("MXA2")

    def stage_a():
        ag_wait("PA1")
        ag_send("P2A1")
        ag_wait("MA2")
        ag_send("M2A2")

    def stage_2b():
        ag_wait("P2B1")
        ag_send("XP2B1")
        ag_wait("M2B2")
        ag_send("XM2B2")

    def stage_xa():
        ag_wait("PXA1")
        ag_send("P2XA1")
        ag_wait("MXA2")
        ag_send("M2XA2")

    def forward(p):
        q = qh[p * PAIR : (p + 1) * PAIR, :]
        s = nt(kh[...], q) * SCALE
        e = jnp.exp(s - jnp.max(s, axis=0, keepdims=True))
        prob = e / jnp.sum(e, axis=0, keepdims=True)
        pt[p] = prob
        at[p] = nn(vt[...], prob.astype(jnp.bfloat16)).astype(jnp.bfloat16)

    def pair_of(dy):
        return lax.rem(y + (dy + 8), 4)

    def prows(pair):
        return pl.ds(pl.multiple_of(pair * PAIR, PAIR), PAIR)

    def add_grad(dy):
        pair = pair_of(dy)
        gw[...] += nn(at[pair], do_all[prows(pair), :])

    def backward(dy):
        pair = pair_of(dy)
        q = qh[prows(pair), :]
        d_f = nn(do_all[prows(pair), :], w_t[...])
        d_b = d_f.astype(jnp.bfloat16)
        d_t = d_b.astype(jnp.float32).T
        row_dot = jnp.sum(d_t * at[pair].astype(jnp.float32), axis=0, keepdims=True)
        prob = pt[pair]
        d_s = (prob * (nt(vh[...], d_b) - row_dot) * SCALE).astype(jnp.bfloat16)
        dk_acc[...] += nn(d_s, q)
        dv_acc[...] += nn(prob.astype(jnp.bfloat16), d_b)
        dq_st[prows(pair), :] = nn(kt[...], d_s).T.astype(jnp.bfloat16)

    def send_rows(j, st, out, dy):
        for dx in range(2):
            r = (dy % 4) * 2 + dx
            t = at_rel(dy, dx)
            if r:
                push(st.at[rows(t), :], out.at[:, cols(me)], back_s.at[j, r], back_r.at[j, r],
                     {"seq": t})

    outs = ((dq_st, dq_out), (dk_st, dk_out), (dv_st, dv_out))

    stage_b()
    stage_x()
    own_k.wait()
    own_v.wait()
    loads["q"].wait()
    a2a_wait(0, qh)
    a2a_wait(1, kh)
    a2a_wait(2, vh)
    kt[...] = kh[...].astype(jnp.float32).T.astype(jnp.bfloat16)
    vt[...] = vh[...].astype(jnp.float32).T.astype(jnp.bfloat16)
    forward(0)
    stage_a()
    forward(1)
    stage_2b()
    forward(2)
    stage_xa()
    forward(3)

    loads["d"].wait()
    ag_wait("XB1")
    ag_wait("XB2")
    add_grad(0)
    backward(0)
    send_rows(0, dq_st, dq_out, 0)

    for name in ("PA2", "PXA2", "XPB1", "XPB2"):
        ag_wait(name)
    add_grad(-1)
    backward(-1)
    send_rows(0, dq_st, dq_out, -1)

    for name in ("MA1", "MXA1", "XMB1", "XMB2"):
        ag_wait(name)
    add_grad(1)
    backward(1)
    send_rows(0, dq_st, dq_out, 1)

    for name in ("P2A1", "M2A2", "P2XA1", "M2XA2", "XP2B1", "XM2B2"):
        ag_wait(name)
    add_grad(2)

    loads["p"].wait()
    new_psi = w_f[...] - 0.02 * gw[...]
    np_out[...] = new_psi
    phi = new_psi + w_f[...] - ps_f[...]
    gw[...] = phi
    phi_b[...] = phi.astype(jnp.bfloat16)
    for i, other in enumerate((nxt, prv)):
        push(phi_b, halo.at[i], halo_s.at[i], halo_r.at[i], {"agent": other})

    backward(2)
    dk_st[...] = dk_acc[...].astype(jnp.bfloat16)
    dv_st[...] = dv_acc[...].astype(jnp.bfloat16)
    for dy in (2, 1, -1, 0):
        send_rows(1, dk_st, dk_out, dy)
        send_rows(2, dv_st, dv_out, dy)
    send_rows(0, dq_st, dq_out, 2)
    own = []
    for j, (st, out) in enumerate(outs):
        own.append(pltpu.make_async_copy(st.at[rows(me), :], out.at[:, cols(me)], own_sem.at[2 + j]))
        own[-1].start()

    for i in range(2):
        arrived(halo.at[i], halo_r.at[i], halo_s.at[i])
    before = mix_ref[0, 0].astype(jnp.float32)
    after = mix_ref[0, 1].astype(jnp.float32)
    nw_out[...] = (
        (16.0 - before - after) * gw[...]
        + before * halo[0].astype(jnp.float32)
        + after * halo[1].astype(jnp.float32)
    ) * 0.0625

    for j, (st, out) in enumerate(outs):
        own[j].wait()
        for r, (dy, dx) in enumerate(rels):
            if r:
                arrived(out.at[:, cols(at_rel(-dy, dx))], back_r.at[j, r], back_s.at[j, r])
    for copy in sent:
        copy.wait_send()


def local(
    queries, key_codes, key_exps, value_codes, value_exps, d_out, out_weight, prev_psi, mixing
):
    bf, f32 = jnp.bfloat16, jnp.float32
    vmem = pl.BlockSpec(memory_space=pltpu.VMEM)
    smem = pl.BlockSpec(memory_space=pltpu.SMEM)
    hbm = pl.BlockSpec(memory_space=pl.ANY)
    outs = pl.pallas_call(
        kernel,
        out_shape=[
            jax.ShapeDtypeStruct((TOK, HD), bf),
            jax.ShapeDtypeStruct((TOK, HD), bf),
            jax.ShapeDtypeStruct((TOK, HD), bf),
            jax.ShapeDtypeStruct((HDIM, D), f32),
            jax.ShapeDtypeStruct((HDIM, D), f32),
        ],
        in_specs=[smem, vmem, vmem] + [hbm] * 6,
        out_specs=[vmem] * 5,
        scratch_shapes=[
            pltpu.VMEM((TOK, HD), bf),
            pltpu.VMEM((TOK, HD), bf),
            pltpu.VMEM((TOK, HD), bf),
            pltpu.VMEM((TOK, HD), bf),
            pltpu.VMEM((TOKENS, HDIM), bf),
            pltpu.VMEM((TOKENS, HDIM), bf),
            pltpu.VMEM((TOKENS, HDIM), bf),
            pltpu.VMEM((HDIM, TOKENS), bf),
            pltpu.VMEM((HDIM, TOKENS), bf),
            pltpu.VMEM((TOKENS, D), bf),
            pltpu.VMEM((HDIM, D), f32),
            pltpu.VMEM((HDIM, D), f32),
            pltpu.VMEM((D, HDIM), bf),
            pltpu.VMEM((N_PAIR, TOKENS, PAIR), f32),
            pltpu.VMEM((N_PAIR, HDIM, PAIR), bf),
            pltpu.VMEM((HDIM, D), f32),
            pltpu.VMEM((TOKENS, HDIM), f32),
            pltpu.VMEM((TOKENS, HDIM), f32),
            pltpu.VMEM((TOKENS, HDIM), bf),
            pltpu.VMEM((TOKENS, HDIM), bf),
            pltpu.VMEM((TOKENS, HDIM), bf),
            pltpu.VMEM((HDIM, D), bf),
            pltpu.VMEM((2, HDIM, D), bf),
            pltpu.SemaphoreType.DMA((6,)),
            pltpu.SemaphoreType.DMA((5,)),
            pltpu.SemaphoreType.DMA((3, N_SEQ)),
            pltpu.SemaphoreType.DMA((3, N_SEQ)),
            pltpu.SemaphoreType.DMA((N_MSG,)),
            pltpu.SemaphoreType.DMA((N_MSG,)),
            pltpu.SemaphoreType.DMA((3, N_SEQ)),
            pltpu.SemaphoreType.DMA((3, N_SEQ)),
            pltpu.SemaphoreType.DMA((2,)),
            pltpu.SemaphoreType.DMA((2,)),
        ],
        compiler_params=pltpu.CompilerParams(
            collective_id=0, has_side_effects=True, vmem_limit_bytes=50 * 1024 * 1024
        ),
        cost_estimate=pl.CostEstimate(
            flops=2 * TOKENS * HDIM * (2 * D + 6 * TOKENS),
            bytes_accessed=8 * 1024 * 1024,
            transcendentals=TOKENS * TOKENS,
        ),
        name="exact_diffusion_step",
    )(
        mixing, key_exps[0], value_exps[0], queries[0], key_codes[0], value_codes[0],
        d_out[0], out_weight[0], prev_psi[0],
    )
    return tuple(out[None] for out in outs)


def solution(mesh):
    rows = P("agent", "seq", None)
    return jax.shard_map(
        local,
        mesh=mesh,
        in_specs=(rows,) * 8 + (P("agent", None),),
        out_specs=(rows,) * 5,
        check_vma=False,
    )
```

```python
import jax
import jax.numpy as jnp
from jax import lax
from jax.experimental import pallas as pl
from jax.experimental.pallas import tpu as pltpu
from jax.sharding import PartitionSpec as P

HEADS = 8
HDIM = 128
TOK = 128
N_SEQ = 8
N_AGENT = 16
TOKENS = N_SEQ * TOK
HD = HEADS * HDIM
D = 2048
PAIR = 2 * TOK
N_PAIR = TOKENS // PAIR
VMEM = 62 * 1024 * 1024
SCALE = HDIM ** (-0.5)
MESH = pl.DeviceIdType.MESH

A1, A2, B1, B2 = (0, 640), (640, 512), (1152, 384), (1536, 512)
PIECES = {"A1": A1, "A2": A2, "B1": B1, "B2": B2}


def _gather_messages():
    msgs = []
    for p in ("B1", "B2", "A1", "A2"):
        msgs.append(("P" + p, "dn", (-1, 0), p))
        msgs.append(("M" + p, "up", (1, 0), p))
        msgs.append(("X" + p, "xp", (0, 1), p))
    for p in ("A1", "A2"):
        msgs.append(("PX" + p, "dn", (-1, 1), p))
        msgs.append(("MX" + p, "up", (1, 1), p))
    msgs.append(("P2A1", "dn", (-2, 0), "A1"))
    msgs.append(("P2XA1", "dn", (-2, 1), "A1"))
    msgs.append(("P2B1", "dn", (-2, 0), "B1"))
    msgs.append(("M2A2", "up", (2, 0), "A2"))
    msgs.append(("M2XA2", "up", (2, 1), "A2"))
    msgs.append(("M2B2", "up", (2, 0), "B2"))
    for p in ("B1", "B2"):
        msgs.append(("XP" + p, "xp", (-1, 1), p))
        msgs.append(("XM" + p, "xp", (1, 1), p))
    msgs.append(("XP2B1", "xp", (-2, 1), "B1"))
    msgs.append(("XM2B2", "xp", (2, 1), "B2"))
    return msgs


MSGS = _gather_messages()
KIND = {m[0]: i for i, m in enumerate(MSGS)}
N_MSG = len(MSGS)


def nt(a, b):
    return lax.dot_general(a, b, (((1,), (1,)), ((), ())), preferred_element_type=jnp.float32)


def nn(a, b):
    return jnp.dot(a, b, preferred_element_type=jnp.float32)


def kernel(
    ke_hbm, ve_hbm, q_hbm, kc_hbm, vc_hbm, do_hbm, w_hbm, ps_hbm,
    dq_out, dk_out, dv_out, np_out, phi_out, halo_out,
    ke_ref, ve_ref, kc_v, vc_v, k_st, v_st, qh, kh, vh, kt, vt, do_all, w_f, ps_f, w_t,
    pt, at, gw, dk_acc, dv_acc, dq_st, dk_st, dv_st, phi_f, phi_b,
    load_sem, own_sem, out_sem, a2a_s, a2a_r, ag_s, ag_r, back_s, back_r, halo_s, halo_r,
):
    me = lax.axis_index("seq")
    agent = lax.axis_index("agent")
    y, x = me // 2, lax.rem(me, 2)

    def at_rel(dy, dx):
        return lax.rem(y + (dy + 8), 4) * 2 + lax.rem(x + dx, 2)

    def rows(block):
        return pl.ds(pl.multiple_of(block * TOK, TOK), TOK)

    def cols(block):
        return pl.ds(pl.multiple_of(block * HDIM, HDIM), HDIM)

    rels = [(dy, dx) for dy in range(4) for dx in range(2)]
    peers = rels[1:]

    loads = {}
    for i, (name, src, dst) in enumerate(
        (
            ("ke", ke_hbm, ke_ref),
            ("k", kc_hbm, kc_v),
            ("ve", ve_hbm, ve_ref),
            ("v", vc_hbm, vc_v),
            ("q", q_hbm.at[:, cols(me)], qh.at[rows(me), :]),
            ("w", w_hbm, w_f),
            ("d", do_hbm, do_all.at[rows(me), :]),
            ("p", ps_hbm, ps_f),
        )
    ):
        loads[name] = pltpu.make_async_copy(src, dst, load_sem.at[i])
        loads[name].start()

    barrier = pltpu.get_barrier_semaphore()
    for dy, dx in peers:
        pl.semaphore_signal(barrier, inc=1, device_id={"seq": at_rel(dy, dx)}, device_id_type=MESH)
    nxt, prv = lax.rem(agent + 1, N_AGENT), lax.rem(agent + N_AGENT - 1, N_AGENT)
    for other in (nxt, prv):
        pl.semaphore_signal(barrier, inc=1, device_id={"agent": other}, device_id_type=MESH)
    pl.semaphore_wait(barrier, len(peers) + 2)

    sent = []

    def push(src, dst, ssem, rsem, target):
        copy = pltpu.make_async_remote_copy(
            src_ref=src, dst_ref=dst, send_sem=ssem, recv_sem=rsem,
            device_id=target, device_id_type=MESH,
        )
        copy.start()
        sent.append(copy)

    def arrived(dst, rsem, ssem):
        pltpu.make_async_remote_copy(
            src_ref=dst, dst_ref=dst, send_sem=ssem, recv_sem=rsem,
            device_id={"seq": at_rel(0, 1)}, device_id_type=MESH,
        ).wait_recv()

    def a2a_send(j, src, dst):
        for r, (dy, dx) in enumerate(rels):
            if r:
                t = at_rel(dy, dx)
                push(src.at[:, cols(t)], dst.at[rows(me), :], a2a_s.at[j, r], a2a_r.at[j, r],
                     {"seq": t})

    def a2a_wait(j, dst):
        for r, (dy, dx) in enumerate(rels):
            if r:
                arrived(dst.at[rows(at_rel(-dy, dx)), :], a2a_r.at[j, r], a2a_s.at[j, r])

    def scaled(codes, expo, out):
        factor = jnp.exp2(expo[...].astype(jnp.float32))
        for h in range(HEADS):
            c = slice(h * HDIM, (h + 1) * HDIM)
            out[:, c] = (codes[:, c].astype(jnp.float32) * factor[0:1, h : h + 1]).astype(
                jnp.bfloat16
            )

    a2a_send(0, q_hbm, qh)
    loads["ke"].wait()
    loads["k"].wait()
    scaled(kc_v, ke_ref, k_st)
    a2a_send(1, k_st, kh)
    loads["ve"].wait()
    loads["v"].wait()
    scaled(vc_v, ve_ref, v_st)
    a2a_send(2, v_st, vh)

    step = {"xp": (0, 1), "up": (1, 0), "dn": (-1, 0)}
    back_to = {"xp": "xp", "up": "dn", "dn": "up"}

    def ag_send(name, own=False):
        kind = KIND[name]
        _, source, (dy, dx), piece = MSGS[kind]
        sy, sx = step[source]
        ty, tx = step[back_to[source]]
        block = at_rel(dy - sy, (dx + sx) % 2)
        first, width = PIECES[piece]
        here = do_all.at[rows(block), pl.ds(first, width)]
        src = do_hbm.at[:, pl.ds(first, width)] if own else here
        push(src, here, ag_s.at[kind], ag_r.at[kind], {"seq": at_rel(ty, tx)})

    def ag_wait(name):
        kind = KIND[name]
        _, _, (dy, dx), piece = MSGS[kind]
        first, width = PIECES[piece]
        arrived(do_all.at[rows(at_rel(dy, dx)), pl.ds(first, width)], ag_r.at[kind], ag_s.at[kind])

    for name in ("PB1", "MB2", "XA1", "PB2", "MB1", "XA2", "PA1", "MA2", "PA2", "MA1", "XB1", "XB2"):
        ag_send(name, own=True)

    own_k = pltpu.make_async_copy(k_st.at[:, cols(me)], kh.at[rows(me), :], own_sem.at[0])
    own_v = pltpu.make_async_copy(v_st.at[:, cols(me)], vh.at[rows(me), :], own_sem.at[1])
    own_k.start()
    own_v.start()

    loads["w"].wait()
    for c in range(0, D, 256):
        w_t[c : c + 256, :] = w_f[:, c : c + 256].T.astype(jnp.bfloat16)
    dk_acc[...] = jnp.zeros_like(dk_acc)
    dv_acc[...] = jnp.zeros_like(dv_acc)
    gw[...] = jnp.zeros_like(gw)

    def stage_b():
        ag_wait("PB1")
        ag_send("P2B1")
        ag_send("XPB1")
        ag_wait("MB2")
        ag_send("M2B2")
        ag_send("XMB2")
        ag_wait("PB2")
        ag_send("XPB2")
        ag_wait("MB1")
        ag_send("XMB1")

    def stage_x():
        ag_wait("XA1")
        ag_send("PXA1")
        ag_send("MXA1")
        ag_wait("XA2")
        ag_send("PXA2")
        ag_send("MXA2")

    def stage_a():
        ag_wait("PA1")
        ag_send("P2A1")
        ag_wait("MA2")
        ag_send("M2A2")

    def stage_2b():
        ag_wait("P2B1")
        ag_send("XP2B1")
        ag_wait("M2B2")
        ag_send("XM2B2")

    def stage_xa():
        ag_wait("PXA1")
        ag_send("P2XA1")
        ag_wait("MXA2")
        ag_send("M2XA2")

    def forward(p):
        q = qh[p * PAIR : (p + 1) * PAIR, :]
        s = nt(kh[...], q) * SCALE
        e = jnp.exp(s - jnp.max(s, axis=0, keepdims=True))
        prob = e / jnp.sum(e, axis=0, keepdims=True)
        pt[p] = prob
        at[p] = nn(vt[...], prob.astype(jnp.bfloat16)).astype(jnp.bfloat16)

    def pair_of(dy):
        return lax.rem(y + (dy + 8), 4)

    def prows(pair):
        return pl.ds(pl.multiple_of(pair * PAIR, PAIR), PAIR)

    def add_grad(dy):
        pair = pair_of(dy)
        gw[...] += nn(at[pair], do_all[prows(pair), :])

    def backward(dy):
        pair = pair_of(dy)
        q = qh[prows(pair), :]
        d_f = nn(do_all[prows(pair), :], w_t[...])
        d_b = d_f.astype(jnp.bfloat16)
        d_t = d_b.astype(jnp.float32).T
        row_dot = jnp.sum(d_t * at[pair].astype(jnp.float32), axis=0, keepdims=True)
        prob = pt[pair]
        d_s = (prob * (nt(vh[...], d_b) - row_dot) * SCALE).astype(jnp.bfloat16)
        dk_acc[...] += nn(d_s, q)
        dv_acc[...] += nn(prob.astype(jnp.bfloat16), d_b)
        dq_st[prows(pair), :] = nn(kt[...], d_s).T.astype(jnp.bfloat16)

    def send_rows(j, st, out, dy):
        for dx in range(2):
            r = (dy % 4) * 2 + dx
            t = at_rel(dy, dx)
            if r:
                push(st.at[rows(t), :], out.at[:, cols(me)], back_s.at[j, r], back_r.at[j, r],
                     {"seq": t})

    outs = ((dq_st, dq_out), (dk_st, dk_out), (dv_st, dv_out))

    stage_b()
    stage_x()
    own_k.wait()
    own_v.wait()
    loads["q"].wait()
    a2a_wait(0, qh)
    a2a_wait(1, kh)
    a2a_wait(2, vh)
    kt[...] = kh[...].astype(jnp.float32).T.astype(jnp.bfloat16)
    vt[...] = vh[...].astype(jnp.float32).T.astype(jnp.bfloat16)
    forward(0)
    stage_a()
    forward(1)
    stage_2b()
    forward(2)
    stage_xa()
    forward(3)

    loads["d"].wait()
    ag_wait("XB1")
    ag_wait("XB2")
    add_grad(0)
    backward(0)
    send_rows(0, dq_st, dq_out, 0)

    for name in ("PA2", "PXA2", "XPB1", "XPB2"):
        ag_wait(name)
    add_grad(-1)
    backward(-1)
    send_rows(0, dq_st, dq_out, -1)

    for name in ("MA1", "MXA1", "XMB1", "XMB2"):
        ag_wait(name)
    add_grad(1)
    backward(1)
    send_rows(0, dq_st, dq_out, 1)

    for name in ("P2A1", "M2A2", "P2XA1", "M2XA2", "XP2B1", "XM2B2"):
        ag_wait(name)
    add_grad(2)

    loads["p"].wait()
    new_psi = w_f[...] - 0.02 * gw[...]
    phi = new_psi + w_f[...] - ps_f[...]
    phi_b[...] = phi.astype(jnp.bfloat16)
    for i, other in enumerate((nxt, prv)):
        push(phi_b, halo_out.at[i], halo_s.at[i], halo_r.at[i], {"agent": other})
    gw[...] = new_psi
    phi_f[...] = phi
    stores = [
        pltpu.make_async_copy(gw, np_out, out_sem.at[0]),
        pltpu.make_async_copy(phi_f, phi_out, out_sem.at[1]),
    ]
    for copy in stores:
        copy.start()

    backward(2)
    dk_st[...] = dk_acc[...].astype(jnp.bfloat16)
    dv_st[...] = dv_acc[...].astype(jnp.bfloat16)
    for dy in (2, 1, -1, 0):
        send_rows(1, dk_st, dk_out, dy)
        send_rows(2, dv_st, dv_out, dy)
    send_rows(0, dq_st, dq_out, 2)
    own = []
    for j, (st, out) in enumerate(outs):
        own.append(pltpu.make_async_copy(st.at[rows(me), :], out.at[:, cols(me)], own_sem.at[2 + j]))
        own[-1].start()

    for i in range(2):
        arrived(halo_out.at[i], halo_r.at[i], halo_s.at[i])
    for copy in stores:
        copy.wait()
    for j, (st, out) in enumerate(outs):
        own[j].wait()
        for r, (dy, dx) in enumerate(rels):
            if r:
                arrived(out.at[:, cols(at_rel(-dy, dx))], back_r.at[j, r], back_s.at[j, r])
    for copy in sent:
        copy.wait_send()


def finish(
    mix_hbm, dq, dk, dv, psi, phi, halo, dq_out, dk_out, dv_out, nw_out, np_out,
    mix, phi_v, halo_v, load_sem, sem,
):
    loads = [
        pltpu.make_async_copy(a, b, load_sem.at[i])
        for i, (a, b) in enumerate(((mix_hbm, mix), (phi, phi_v), (halo, halo_v)))
    ]
    for copy in loads:
        copy.start()
    copies = [
        pltpu.make_async_copy(a, b, sem.at[i])
        for i, (a, b) in enumerate(((psi, np_out), (dq, dq_out), (dk, dk_out), (dv, dv_out)))
    ]
    for copy in copies:
        copy.start()
    for copy in loads:
        copy.wait()
    before = mix[0, 0].astype(jnp.float32)
    after = mix[0, 1].astype(jnp.float32)
    phi_v[...] = (
        (16.0 - before - after) * phi_v[...]
        + before * halo_v[0].astype(jnp.float32)
        + after * halo_v[1].astype(jnp.float32)
    ) * 0.0625
    copies.append(pltpu.make_async_copy(phi_v, nw_out, sem.at[4]))
    copies[-1].start()
    for copy in copies:
        copy.wait()


def local(
    queries, key_codes, key_exps, value_codes, value_exps, d_out, out_weight, prev_psi, mixing
):
    bf, f32 = jnp.bfloat16, jnp.float32
    hbm = pl.BlockSpec(memory_space=pltpu.HBM)
    small, large = jax.ShapeDtypeStruct((TOK, HD), bf), jax.ShapeDtypeStruct((HDIM, D), f32)
    *grads, psi, phi, halo = pl.pallas_call(
        kernel,
        out_shape=[small] * 3 + [large] * 2 + [jax.ShapeDtypeStruct((2, HDIM, D), bf)],
        in_specs=[hbm] * 8,
        out_specs=[hbm] * 6,
        scratch_shapes=[
            pltpu.VMEM((1, HEADS), jnp.int32),
            pltpu.VMEM((1, HEADS), jnp.int32),
            pltpu.VMEM((TOK, HD), bf),
            pltpu.VMEM((TOK, HD), bf),
            pltpu.VMEM((TOK, HD), bf),
            pltpu.VMEM((TOK, HD), bf),
            pltpu.VMEM((TOKENS, HDIM), bf),
            pltpu.VMEM((TOKENS, HDIM), bf),
            pltpu.VMEM((TOKENS, HDIM), bf),
            pltpu.VMEM((HDIM, TOKENS), bf),
            pltpu.VMEM((HDIM, TOKENS), bf),
            pltpu.VMEM((TOKENS, D), bf),
            pltpu.VMEM((HDIM, D), f32),
            pltpu.VMEM((HDIM, D), f32),
            pltpu.VMEM((D, HDIM), bf),
            pltpu.VMEM((N_PAIR, TOKENS, PAIR), f32),
            pltpu.VMEM((N_PAIR, HDIM, PAIR), bf),
            pltpu.VMEM((HDIM, D), f32),
            pltpu.VMEM((TOKENS, HDIM), f32),
            pltpu.VMEM((TOKENS, HDIM), f32),
            pltpu.VMEM((TOKENS, HDIM), bf),
            pltpu.VMEM((TOKENS, HDIM), bf),
            pltpu.VMEM((TOKENS, HDIM), bf),
            pltpu.VMEM((HDIM, D), f32),
            pltpu.VMEM((HDIM, D), bf),
            pltpu.SemaphoreType.DMA((8,)),
            pltpu.SemaphoreType.DMA((5,)),
            pltpu.SemaphoreType.DMA((2,)),
            pltpu.SemaphoreType.DMA((3, N_SEQ)),
            pltpu.SemaphoreType.DMA((3, N_SEQ)),
            pltpu.SemaphoreType.DMA((N_MSG,)),
            pltpu.SemaphoreType.DMA((N_MSG,)),
            pltpu.SemaphoreType.DMA((3, N_SEQ)),
            pltpu.SemaphoreType.DMA((3, N_SEQ)),
            pltpu.SemaphoreType.DMA((2,)),
            pltpu.SemaphoreType.DMA((2,)),
        ],
        compiler_params=pltpu.CompilerParams(
            collective_id=0, has_side_effects=True, vmem_limit_bytes=VMEM
        ),
        cost_estimate=pl.CostEstimate(
            flops=2 * TOKENS * HDIM * (2 * D + 6 * TOKENS),
            bytes_accessed=8 * 1024 * 1024,
            transcendentals=TOKENS * TOKENS,
        ),
        name="exact_diffusion_step",
    )(
        key_exps[0], value_exps[0], queries[0], key_codes[0], value_codes[0],
        d_out[0], out_weight[0], prev_psi[0],
    )
    outs = pl.pallas_call(
        finish,
        out_shape=[small] * 3 + [large] * 2,
        in_specs=[hbm] * 7,
        out_specs=[hbm] * 5,
        scratch_shapes=[
            pltpu.SMEM((1, 2), jnp.int32),
            pltpu.VMEM((HDIM, D), f32),
            pltpu.VMEM((2, HDIM, D), bf),
            pltpu.SemaphoreType.DMA((3,)),
            pltpu.SemaphoreType.DMA((5,)),
        ],
        compiler_params=pltpu.CompilerParams(vmem_limit_bytes=VMEM),
        name="finish",
    )(mixing, *grads, psi, phi, halo)
    return tuple(out[None] for out in outs)


def solution(mesh):
    rows = P("agent", "seq", None)
    return jax.shard_map(
        local,
        mesh=mesh,
        in_specs=(rows,) * 8 + (P("agent", None),),
        out_specs=(rows,) * 5,
        check_vma=False,
    )
```

```python
import jax
import jax.numpy as jnp
from jax import lax
from jax.experimental import pallas as pl
from jax.experimental.pallas import tpu as pltpu
from jax.sharding import PartitionSpec as P

HEADS = 8
HDIM = 128
TOK = 128
N_SEQ = 8
N_AGENT = 16
TOKENS = N_SEQ * TOK
HD = HEADS * HDIM
D = 2048
PAIR = 2 * TOK
N_PAIR = TOKENS // PAIR
VMEM = 62 * 1024 * 1024
CHUNK = 32
N_CHUNK = HDIM // CHUNK
SCALE = HDIM ** (-0.5)
MESH = pl.DeviceIdType.MESH

A1, A2, B1, B2 = (0, 640), (640, 640), (1280, 384), (1664, 384)
PIECES = {"A1": A1, "A2": A2, "B1": B1, "B2": B2}


def _gather_messages():
    msgs = []
    for p in ("B1", "B2", "A1", "A2"):
        msgs.append(("P" + p, "dn", (-1, 0), p))
        msgs.append(("M" + p, "up", (1, 0), p))
        msgs.append(("X" + p, "xp", (0, 1), p))
    for p in ("A1", "A2"):
        msgs.append(("PX" + p, "dn", (-1, 1), p))
        msgs.append(("MX" + p, "up", (1, 1), p))
    msgs.append(("P2A1", "dn", (-2, 0), "A1"))
    msgs.append(("P2XA1", "dn", (-2, 1), "A1"))
    msgs.append(("P2B1", "dn", (-2, 0), "B1"))
    msgs.append(("M2A2", "up", (2, 0), "A2"))
    msgs.append(("M2XA2", "up", (2, 1), "A2"))
    msgs.append(("M2B2", "up", (2, 0), "B2"))
    for p in ("B1", "B2"):
        msgs.append(("XP" + p, "xp", (-1, 1), p))
        msgs.append(("XM" + p, "xp", (1, 1), p))
    msgs.append(("XP2B1", "xp", (-2, 1), "B1"))
    msgs.append(("XM2B2", "xp", (2, 1), "B2"))
    return msgs


MSGS = _gather_messages()
KIND = {m[0]: i for i, m in enumerate(MSGS)}
N_MSG = len(MSGS)


def nt(a, b):
    return lax.dot_general(a, b, (((1,), (1,)), ((), ())), preferred_element_type=jnp.float32)


def nn(a, b):
    return jnp.dot(a, b, preferred_element_type=jnp.float32)


def kernel(
    ke_hbm, ve_hbm, q_hbm, kc_hbm, vc_hbm, do_hbm, w_hbm, ps_hbm,
    dq_out, dk_out, dv_out, np_out, phi_out, halo_out,
    ke_ref, ve_ref, kc_v, vc_v, k_st, v_st, qh, kh, vh, kt, vt, do_all, w_f, ps_f, w_t,
    pt, at, gw, dk_acc, dv_acc, dq_st, dk_st, dv_st, phi_f, phi_b,
    load_sem, own_sem, out_sem, a2a_s, a2a_r, ag_s, ag_r, back_s, back_r, halo_s, halo_r, turn,
):
    me = lax.axis_index("seq")
    agent = lax.axis_index("agent")
    y, x = me // 2, lax.rem(me, 2)

    def at_rel(dy, dx):
        return lax.rem(y + (dy + 8), 4) * 2 + lax.rem(x + dx, 2)

    def rows(block):
        return pl.ds(pl.multiple_of(block * TOK, TOK), TOK)

    def cols(block):
        return pl.ds(pl.multiple_of(block * HDIM, HDIM), HDIM)

    rels = [(dy, dx) for dy in range(4) for dx in range(2)]
    peers = rels[1:]

    loads = {}
    for i, (name, src, dst) in enumerate(
        (
            ("ke", ke_hbm, ke_ref),
            ("k", kc_hbm, kc_v),
            ("ve", ve_hbm, ve_ref),
            ("v", vc_hbm, vc_v),
            ("q", q_hbm.at[:, cols(me)], qh.at[rows(me), :]),
            ("w", w_hbm, w_f),
            ("d", do_hbm, do_all.at[rows(me), :]),
            ("p", ps_hbm, ps_f),
        )
    ):
        loads[name] = pltpu.make_async_copy(src, dst, load_sem.at[i])
        loads[name].start()

    barrier = pltpu.get_barrier_semaphore()
    for dy, dx in peers:
        pl.semaphore_signal(barrier, inc=1, device_id={"seq": at_rel(dy, dx)}, device_id_type=MESH)
    nxt, prv = lax.rem(agent + 1, N_AGENT), lax.rem(agent + N_AGENT - 1, N_AGENT)
    for other in (nxt, prv):
        pl.semaphore_signal(barrier, inc=1, device_id={"agent": other}, device_id_type=MESH)
    def scaled(codes, expo, out):
        factor = jnp.exp2(expo[...].astype(jnp.float32))
        for h in range(HEADS):
            c = slice(h * HDIM, (h + 1) * HDIM)
            out[:, c] = (codes[:, c].astype(jnp.float32) * factor[0:1, h : h + 1]).astype(
                jnp.bfloat16
            )

    for codes, expo, out, a, b in (
        (kc_v, ke_ref, k_st, "ke", "k"),
        (vc_v, ve_ref, v_st, "ve", "v"),
    ):
        loads[a].wait()
        loads[b].wait()
        scaled(codes, expo, out)
    pl.semaphore_wait(barrier, len(peers) + 2)

    sent = []

    place = lax.rem(agent, 8)
    ends = jnp.logical_or(place == 0, place == 7)
    mates = jnp.logical_or(place == 1, place == 6)
    mate = agent + 1 - 2 * lax.rem(agent, 2)

    def push(src, dst, ssem, rsem, target):
        copy = pltpu.make_async_remote_copy(
            src_ref=src, dst_ref=dst, send_sem=ssem, recv_sem=rsem,
            device_id=target, device_id_type=MESH,
        )
        copy.start()
        sent.append(copy)

    def arrived(dst, rsem, ssem):
        pltpu.make_async_remote_copy(
            src_ref=dst, dst_ref=dst, send_sem=ssem, recv_sem=rsem,
            device_id={"seq": at_rel(0, 1)}, device_id_type=MESH,
        ).wait_recv()

    def a2a_send(j, src, dst):
        for r, (dy, dx) in enumerate(rels):
            if r:
                t = at_rel(dy, dx)
                push(src.at[:, cols(t)], dst.at[rows(me), :], a2a_s.at[j, r], a2a_r.at[j, r],
                     {"seq": t})

    def a2a_wait(j, dst):
        for r, (dy, dx) in enumerate(rels):
            if r:
                arrived(dst.at[rows(at_rel(-dy, dx)), :], a2a_r.at[j, r], a2a_s.at[j, r])

    a2a_send(0, q_hbm, qh)
    a2a_send(1, k_st, kh)
    a2a_send(2, v_st, vh)

    step = {"xp": (0, 1), "up": (1, 0), "dn": (-1, 0)}
    back_to = {"xp": "xp", "up": "dn", "dn": "up"}

    def ag_send(name, own=False):
        kind = KIND[name]
        _, source, (dy, dx), piece = MSGS[kind]
        sy, sx = step[source]
        ty, tx = step[back_to[source]]
        block = at_rel(dy - sy, (dx + sx) % 2)
        first, width = PIECES[piece]
        here = do_all.at[rows(block), pl.ds(first, width)]
        src = do_hbm.at[:, pl.ds(first, width)] if own else here
        push(src, here, ag_s.at[kind], ag_r.at[kind], {"seq": at_rel(ty, tx)})

    def ag_wait(name):
        kind = KIND[name]
        _, _, (dy, dx), piece = MSGS[kind]
        first, width = PIECES[piece]
        arrived(do_all.at[rows(at_rel(dy, dx)), pl.ds(first, width)], ag_r.at[kind], ag_s.at[kind])

    @pl.when(mates)
    def _():
        pl.semaphore_wait(turn, 1)

    for name in ("PB1", "MB2", "XA1", "PB2", "MB1", "XA2", "PA1", "MA2", "PA2", "MA1", "XB1", "XB2"):
        ag_send(name, own=True)

    own_k = pltpu.make_async_copy(k_st.at[:, cols(me)], kh.at[rows(me), :], own_sem.at[0])
    own_v = pltpu.make_async_copy(v_st.at[:, cols(me)], vh.at[rows(me), :], own_sem.at[1])
    own_k.start()
    own_v.start()

    loads["w"].wait()
    for c in range(0, D, 256):
        w_t[c : c + 256, :] = w_f[:, c : c + 256].T.astype(jnp.bfloat16)
    dk_acc[...] = jnp.zeros_like(dk_acc)
    dv_acc[...] = jnp.zeros_like(dv_acc)
    gw[...] = jnp.zeros_like(gw)

    def stage_b():
        ag_wait("PB1")
        ag_send("P2B1")
        ag_send("XPB1")
        ag_wait("MB2")
        ag_send("M2B2")
        ag_send("XMB2")
        ag_wait("PB2")
        ag_send("XPB2")
        ag_wait("MB1")
        ag_send("XMB1")

    def stage_x():
        ag_wait("XA1")
        ag_send("PXA1")
        ag_send("MXA1")
        ag_wait("XA2")
        ag_send("PXA2")
        ag_send("MXA2")

    def stage_a():
        ag_wait("PA1")
        ag_send("P2A1")
        ag_wait("MA2")
        ag_send("M2A2")

    def stage_2b():
        ag_wait("P2B1")
        ag_send("XP2B1")
        ag_wait("M2B2")
        ag_send("XM2B2")

    def stage_xa():
        ag_wait("PXA1")
        ag_send("P2XA1")
        ag_wait("MXA2")
        ag_send("M2XA2")

    def forward(p):
        q = qh[p * PAIR : (p + 1) * PAIR, :]
        s = nt(kh[...], q) * SCALE
        e = jnp.exp(s - jnp.max(s, axis=0, keepdims=True))
        prob = e / jnp.sum(e, axis=0, keepdims=True)
        pt[p] = prob
        at[p] = nn(vt[...], prob.astype(jnp.bfloat16)).astype(jnp.bfloat16)

    def pair_of(dy):
        return lax.rem(y + (dy + 8), 4)

    def prows(pair):
        return pl.ds(pl.multiple_of(pair * PAIR, PAIR), PAIR)

    def add_grad(dy):
        pair = pair_of(dy)
        gw[...] += nn(at[pair], do_all[prows(pair), :])

    def send_rows(j, st, out, dy):
        for dx in range(2):
            r = (dy % 4) * 2 + dx
            t = at_rel(dy, dx)
            if r:
                push(st.at[rows(t), :], out.at[:, cols(me)], back_s.at[j, r], back_r.at[j, r],
                     {"seq": t})

    def backward(dy, last=False):
        pair = pair_of(dy)
        q = qh[prows(pair), :]
        d_f = nn(do_all[prows(pair), :], w_t[...])
        d_b = d_f.astype(jnp.bfloat16)
        d_t = d_b.astype(jnp.float32).T
        row_dot = jnp.sum(d_t * at[pair].astype(jnp.float32), axis=0, keepdims=True)
        prob = pt[pair]
        if last:
            dv_st[...] = (dv_acc[...] + nn(prob.astype(jnp.bfloat16), d_b)).astype(jnp.bfloat16)
            for away in (2, 1, -1, 0):
                send_rows(2, dv_st, dv_out, away)
        else:
            dv_acc[...] += nn(prob.astype(jnp.bfloat16), d_b)
        d_s = (prob * (nt(vh[...], d_b) - row_dot) * SCALE).astype(jnp.bfloat16)
        if last:
            dk_st[...] = (dk_acc[...] + nn(d_s, q)).astype(jnp.bfloat16)
            for away in (2, 1, -1, 0):
                send_rows(1, dk_st, dk_out, away)
        else:
            dk_acc[...] += nn(d_s, q)
        dq_st[prows(pair), :] = nn(kt[...], d_s).T.astype(jnp.bfloat16)
        if last:
            send_rows(0, dq_st, dq_out, 2)

    outs = ((dq_st, dq_out), (dk_st, dk_out), (dv_st, dv_out))

    stage_b()
    stage_x()

    @pl.when(ends)
    def _():
        pl.semaphore_signal(turn, inc=1, device_id={"agent": mate}, device_id_type=MESH)

    own_k.wait()
    own_v.wait()
    loads["q"].wait()
    a2a_wait(0, qh)
    a2a_wait(1, kh)
    a2a_wait(2, vh)
    kt[...] = kh[...].astype(jnp.float32).T.astype(jnp.bfloat16)
    vt[...] = vh[...].astype(jnp.float32).T.astype(jnp.bfloat16)
    forward(0)
    stage_a()
    forward(1)
    stage_2b()
    forward(2)
    stage_xa()
    forward(3)

    loads["d"].wait()
    loads["p"].wait()
    ps_f[...] = 2.0 * w_f[...] - ps_f[...]
    ag_wait("XB1")
    ag_wait("XB2")
    add_grad(0)
    backward(0)
    send_rows(0, dq_st, dq_out, 0)

    for name in ("PA2", "PXA2", "XPB1", "XPB2"):
        ag_wait(name)
    add_grad(-1)
    backward(-1)
    send_rows(0, dq_st, dq_out, -1)

    for name in ("MA1", "MXA1", "XMB1", "XMB2"):
        ag_wait(name)
    add_grad(1)
    backward(1)
    send_rows(0, dq_st, dq_out, 1)

    for name in ("P2A1", "M2A2", "P2XA1", "M2XA2", "XP2B1", "XM2B2"):
        ag_wait(name)
    last = pair_of(2)
    for half in range(2):
        for c in range(half * D // 2, (half + 1) * D // 2, 256):
            g = gw[:, c : c + 256] + nn(at[last], do_all[prows(last), c : c + 256])
            gw[:, c : c + 256] = g
            phi = ps_f[:, c : c + 256] - 0.02 * g
            phi_f[:, c : c + 256] = phi
            phi_b[:, c : c + 256] = phi.astype(jnp.bfloat16)
        part = pl.ds(half * D // 2, D // 2)
        for i, other in enumerate((nxt, prv)):
            push(phi_b.at[:, part], halo_out.at[i, :, part], halo_s.at[i, half], halo_r.at[i, half],
                 {"agent": other})

    backward(2, last=True)
    gw[...] = w_f[...] - 0.02 * gw[...]
    stores = [
        pltpu.make_async_copy(gw, np_out, out_sem.at[0]),
        pltpu.make_async_copy(phi_f, phi_out, out_sem.at[1]),
    ]
    for copy in stores:
        copy.start()
    own = []
    for j, (st, out) in enumerate(outs):
        own.append(pltpu.make_async_copy(st.at[rows(me), :], out.at[:, cols(me)], own_sem.at[2 + j]))
        own[-1].start()

    for half in range(2):
        part = pl.ds(half * D // 2, D // 2)
        for i in range(2):
            arrived(halo_out.at[i, :, part], halo_r.at[i, half], halo_s.at[i, half])
    for copy in stores:
        copy.wait()
    for j, (st, out) in enumerate(outs):
        own[j].wait()
        for r, (dy, dx) in enumerate(rels):
            if r:
                arrived(out.at[:, cols(at_rel(-dy, dx))], back_r.at[j, r], back_s.at[j, r])
    for copy in sent:
        copy.wait_send()


def finish(
    mix_hbm, dq, dk, dv, psi, phi, halo, dq_out, dk_out, dv_out, nw_out, np_out,
    mix, dq_v, dk_v, dv_v, psi_v, phi_v, halo_v, load_sem, phi_sem, sem, nw_sem,
):
    mix_load = pltpu.make_async_copy(mix_hbm, mix, load_sem.at[0])
    mix_load.start()
    chunks = []
    for c in range(N_CHUNK):
        r = pl.ds(c * CHUNK, CHUNK)
        chunks.append(
            (
                pltpu.make_async_copy(phi.at[r, :], phi_v.at[r, :], phi_sem.at[0, c]),
                pltpu.make_async_copy(halo.at[:, r, :], halo_v.at[:, r, :], phi_sem.at[1, c]),
                pltpu.make_async_copy(phi_v.at[r, :], nw_out.at[r, :], nw_sem.at[c]),
            )
        )
        chunks[-1][0].start()
        chunks[-1][1].start()
    rest = []
    for i, (a, b, out) in enumerate(
        ((psi, psi_v, np_out), (dq, dq_v, dq_out), (dk, dk_v, dk_out), (dv, dv_v, dv_out))
    ):
        rest.append(
            (
                pltpu.make_async_copy(a, b, load_sem.at[i + 1]),
                pltpu.make_async_copy(b, out, sem.at[i]),
            )
        )
        rest[-1][0].start()
    mix_load.wait()
    before = mix[0, 0].astype(jnp.float32)
    after = mix[0, 1].astype(jnp.float32)
    for c, (own, others, store) in enumerate(chunks):
        r = slice(c * CHUNK, (c + 1) * CHUNK)
        own.wait()
        others.wait()
        phi_v[r, :] = (
            (16.0 - before - after) * phi_v[r, :]
            + before * halo_v[0, r, :].astype(jnp.float32)
            + after * halo_v[1, r, :].astype(jnp.float32)
        ) * 0.0625
        store.start()
    for load, store in rest:
        load.wait()
        store.start()
    for _, _, store in chunks:
        store.wait()
    for _, store in rest:
        store.wait()


def local(
    queries, key_codes, key_exps, value_codes, value_exps, d_out, out_weight, prev_psi, mixing
):
    bf, f32 = jnp.bfloat16, jnp.float32
    hbm = pl.BlockSpec(memory_space=pltpu.HBM)
    small, large = jax.ShapeDtypeStruct((TOK, HD), bf), jax.ShapeDtypeStruct((HDIM, D), f32)
    *grads, psi, phi, halo = pl.pallas_call(
        kernel,
        out_shape=[small] * 3 + [large] * 2 + [jax.ShapeDtypeStruct((2, HDIM, D), bf)],
        in_specs=[hbm] * 8,
        out_specs=[hbm] * 6,
        scratch_shapes=[
            pltpu.VMEM((1, HEADS), jnp.int32),
            pltpu.VMEM((1, HEADS), jnp.int32),
            pltpu.VMEM((TOK, HD), bf),
            pltpu.VMEM((TOK, HD), bf),
            pltpu.VMEM((TOK, HD), bf),
            pltpu.VMEM((TOK, HD), bf),
            pltpu.VMEM((TOKENS, HDIM), bf),
            pltpu.VMEM((TOKENS, HDIM), bf),
            pltpu.VMEM((TOKENS, HDIM), bf),
            pltpu.VMEM((HDIM, TOKENS), bf),
            pltpu.VMEM((HDIM, TOKENS), bf),
            pltpu.VMEM((TOKENS, D), bf),
            pltpu.VMEM((HDIM, D), f32),
            pltpu.VMEM((HDIM, D), f32),
            pltpu.VMEM((D, HDIM), bf),
            pltpu.VMEM((N_PAIR, TOKENS, PAIR), f32),
            pltpu.VMEM((N_PAIR, HDIM, PAIR), bf),
            pltpu.VMEM((HDIM, D), f32),
            pltpu.VMEM((TOKENS, HDIM), f32),
            pltpu.VMEM((TOKENS, HDIM), f32),
            pltpu.VMEM((TOKENS, HDIM), bf),
            pltpu.VMEM((TOKENS, HDIM), bf),
            pltpu.VMEM((TOKENS, HDIM), bf),
            pltpu.VMEM((HDIM, D), f32),
            pltpu.VMEM((HDIM, D), bf),
            pltpu.SemaphoreType.DMA((8,)),
            pltpu.SemaphoreType.DMA((5,)),
            pltpu.SemaphoreType.DMA((2,)),
            pltpu.SemaphoreType.DMA((3, N_SEQ)),
            pltpu.SemaphoreType.DMA((3, N_SEQ)),
            pltpu.SemaphoreType.DMA((N_MSG,)),
            pltpu.SemaphoreType.DMA((N_MSG,)),
            pltpu.SemaphoreType.DMA((3, N_SEQ)),
            pltpu.SemaphoreType.DMA((3, N_SEQ)),
            pltpu.SemaphoreType.DMA((2, 2)),
            pltpu.SemaphoreType.DMA((2, 2)),
            pltpu.SemaphoreType.REGULAR,
        ],
        compiler_params=pltpu.CompilerParams(
            collective_id=0, has_side_effects=True, vmem_limit_bytes=VMEM
        ),
        cost_estimate=pl.CostEstimate(
            flops=2 * TOKENS * HDIM * (2 * D + 6 * TOKENS),
            bytes_accessed=8 * 1024 * 1024,
            transcendentals=TOKENS * TOKENS,
        ),
        name="exact_diffusion_step",
    )(
        key_exps[0], value_exps[0], queries[0], key_codes[0], value_codes[0],
        d_out[0], out_weight[0], prev_psi[0],
    )
    outs = pl.pallas_call(
        finish,
        out_shape=[small] * 3 + [large] * 2,
        in_specs=[hbm] * 7,
        out_specs=[hbm] * 5,
        scratch_shapes=[
            pltpu.SMEM((1, 2), jnp.int32),
            pltpu.VMEM((TOK, HD), bf),
            pltpu.VMEM((TOK, HD), bf),
            pltpu.VMEM((TOK, HD), bf),
            pltpu.VMEM((HDIM, D), f32),
            pltpu.VMEM((HDIM, D), f32),
            pltpu.VMEM((2, HDIM, D), bf),
            pltpu.SemaphoreType.DMA((5,)),
            pltpu.SemaphoreType.DMA((2, N_CHUNK)),
            pltpu.SemaphoreType.DMA((4,)),
            pltpu.SemaphoreType.DMA((N_CHUNK,)),
        ],
        compiler_params=pltpu.CompilerParams(vmem_limit_bytes=VMEM),
        name="finish",
    )(mixing, *grads, psi, phi, halo)
    return tuple(out[None] for out in outs)


def solution(mesh):
    rows = P("agent", "seq", None)
    return jax.shard_map(
        local,
        mesh=mesh,
        in_specs=(rows,) * 8 + (P("agent", None),),
        out_specs=(rows,) * 5,
        check_vma=False,
    )
```

```python
import jax
import jax.numpy as jnp
from jax import lax
from jax.experimental import pallas as pl
from jax.experimental.pallas import tpu as pltpu
from jax.sharding import PartitionSpec as P

HEADS = 8
HDIM = 128
TOK = 128
N_SEQ = 8
N_AGENT = 16
TOKENS = N_SEQ * TOK
HD = HEADS * HDIM
D = 2048
PAIR = 2 * TOK
VMEM = 62 * 1024 * 1024
SCALE = HDIM ** (-0.5)
MESH = pl.DeviceIdType.MESH

A1, A2, B1, B2 = (0, 640), (640, 640), (1280, 384), (1664, 384)
PIECES = {"A1": A1, "A2": A2, "B1": B1, "B2": B2}


def _gather_messages():
    msgs = []
    for p in ("B1", "B2", "A1", "A2"):
        msgs.append(("P" + p, "dn", (-1, 0), p))
        msgs.append(("M" + p, "up", (1, 0), p))
        msgs.append(("X" + p, "xp", (0, 1), p))
    for p in ("A1", "A2"):
        msgs.append(("PX" + p, "dn", (-1, 1), p))
        msgs.append(("MX" + p, "up", (1, 1), p))
    msgs.append(("P2A1", "dn", (-2, 0), "A1"))
    msgs.append(("P2XA1", "dn", (-2, 1), "A1"))
    msgs.append(("P2B1", "dn", (-2, 0), "B1"))
    msgs.append(("M2A2", "up", (2, 0), "A2"))
    msgs.append(("M2XA2", "up", (2, 1), "A2"))
    msgs.append(("M2B2", "up", (2, 0), "B2"))
    for p in ("B1", "B2"):
        msgs.append(("XP" + p, "xp", (-1, 1), p))
        msgs.append(("XM" + p, "xp", (1, 1), p))
    msgs.append(("XP2B1", "xp", (-2, 1), "B1"))
    msgs.append(("XM2B2", "xp", (2, 1), "B2"))
    return msgs


MSGS = _gather_messages()
KIND = {m[0]: i for i, m in enumerate(MSGS)}
N_MSG = len(MSGS)
LAST = (("XP2B1", "B1"), ("XM2B2", "B2"), ("P2XA1", "A1"), ("M2XA2", "A2"))


def nt(a, b):
    return lax.dot_general(a, b, (((1,), (1,)), ((), ())), preferred_element_type=jnp.float32)


def nn(a, b):
    return jnp.dot(a, b, preferred_element_type=jnp.float32)


def kernel(
    mix_hbm, ke_hbm, ve_hbm, q_hbm, kc_hbm, vc_hbm, do_hbm, w_hbm, ps_hbm,
    dq_out, dk_out, dv_out, nw_out, np_out,
    mix_ref, ke_ref, ve_ref, kc_v, vc_v, k_st, v_st, qh, kh, vh, kt, vt, do_all, w_f, ps_f, w_t,
    pt, at, gw, dk_acc, dv_acc, dq_st, dk_st, dv_st, phi_f, phi_b, halo,
    load_sem, own_sem, out_sem, a2a_s, a2a_r, ag_s, ag_r, back_s, back_r, halo_s, halo_r, turn,
):
    me = lax.axis_index("seq")
    agent = lax.axis_index("agent")
    y, x = me // 2, lax.rem(me, 2)

    def at_rel(dy, dx):
        return lax.rem(y + (dy + 8), 4) * 2 + lax.rem(x + dx, 2)

    def rows(block):
        return pl.ds(pl.multiple_of(block * TOK, TOK), TOK)

    def cols(block):
        return pl.ds(pl.multiple_of(block * HDIM, HDIM), HDIM)

    rels = [(dy, dx) for dy in range(4) for dx in range(2)]
    peers = rels[1:]

    loads = {}
    for i, (name, src, dst) in enumerate(
        (
            ("ke", ke_hbm, ke_ref),
            ("k", kc_hbm, kc_v),
            ("ve", ve_hbm, ve_ref),
            ("v", vc_hbm, vc_v),
            ("q", q_hbm.at[:, cols(me)], qh.at[rows(me), :]),
            ("w", w_hbm, w_f),
            ("d", do_hbm, do_all.at[rows(me), :]),
            ("p", ps_hbm, ps_f),
            ("m", mix_hbm, mix_ref),
        )
    ):
        loads[name] = pltpu.make_async_copy(src, dst, load_sem.at[i])
        loads[name].start()

    barrier = pltpu.get_barrier_semaphore()
    for dy, dx in peers:
        pl.semaphore_signal(barrier, inc=1, device_id={"seq": at_rel(dy, dx)}, device_id_type=MESH)
    nxt, prv = lax.rem(agent + 1, N_AGENT), lax.rem(agent + N_AGENT - 1, N_AGENT)
    for other in (nxt, prv):
        pl.semaphore_signal(barrier, inc=1, device_id={"agent": other}, device_id_type=MESH)
    def scaled(codes, expo, out):
        factor = jnp.exp2(expo[...].astype(jnp.float32))
        for h in range(HEADS):
            c = slice(h * HDIM, (h + 1) * HDIM)
            out[:, c] = (codes[:, c].astype(jnp.float32) * factor[0:1, h : h + 1]).astype(
                jnp.bfloat16
            )

    for codes, expo, out, a, b in (
        (kc_v, ke_ref, k_st, "ke", "k"),
        (vc_v, ve_ref, v_st, "ve", "v"),
    ):
        loads[a].wait()
        loads[b].wait()
        scaled(codes, expo, out)
    pl.semaphore_wait(barrier, len(peers) + 2)

    sent = []

    place = lax.rem(agent, 8)
    ends = jnp.logical_or(place == 0, place == 7)
    mates = jnp.logical_or(place == 1, place == 6)
    mate = agent + 1 - 2 * lax.rem(agent, 2)

    def push(src, dst, ssem, rsem, target):
        copy = pltpu.make_async_remote_copy(
            src_ref=src, dst_ref=dst, send_sem=ssem, recv_sem=rsem,
            device_id=target, device_id_type=MESH,
        )
        copy.start()
        sent.append(copy)

    def arrived(dst, rsem, ssem):
        pltpu.make_async_remote_copy(
            src_ref=dst, dst_ref=dst, send_sem=ssem, recv_sem=rsem,
            device_id={"seq": at_rel(0, 1)}, device_id_type=MESH,
        ).wait_recv()

    def a2a_send(j, src, dst):
        for r, (dy, dx) in enumerate(rels):
            if r:
                t = at_rel(dy, dx)
                push(src.at[:, cols(t)], dst.at[rows(me), :], a2a_s.at[j, r], a2a_r.at[j, r],
                     {"seq": t})

    def a2a_wait(j, dst):
        for r, (dy, dx) in enumerate(rels):
            if r:
                arrived(dst.at[rows(at_rel(-dy, dx)), :], a2a_r.at[j, r], a2a_s.at[j, r])

    a2a_send(0, q_hbm, qh)
    a2a_send(1, k_st, kh)
    a2a_send(2, v_st, vh)

    step = {"xp": (0, 1), "up": (1, 0), "dn": (-1, 0)}
    back_to = {"xp": "xp", "up": "dn", "dn": "up"}

    def ag_send(name, own=False):
        kind = KIND[name]
        _, source, (dy, dx), piece = MSGS[kind]
        sy, sx = step[source]
        ty, tx = step[back_to[source]]
        block = at_rel(dy - sy, (dx + sx) % 2)
        first, width = PIECES[piece]
        here = do_all.at[rows(block), pl.ds(first, width)]
        src = do_hbm.at[:, pl.ds(first, width)] if own else here
        push(src, here, ag_s.at[kind], ag_r.at[kind], {"seq": at_rel(ty, tx)})

    def ag_wait(*names):
        for name in names:
            kind = KIND[name]
            _, _, (dy, dx), piece = MSGS[kind]
            first, width = PIECES[piece]
            here = do_all.at[rows(at_rel(dy, dx)), pl.ds(first, width)]
            arrived(here, ag_r.at[kind], ag_s.at[kind])

    @pl.when(mates)
    def _():
        pl.semaphore_wait(turn, 1)

    for name in ("PB1", "MB2", "XA1", "PB2", "MB1", "XA2", "PA1", "MA2", "PA2", "MA1", "XB1", "XB2"):
        ag_send(name, own=True)

    own_k = pltpu.make_async_copy(k_st.at[:, cols(me)], kh.at[rows(me), :], own_sem.at[0])
    own_v = pltpu.make_async_copy(v_st.at[:, cols(me)], vh.at[rows(me), :], own_sem.at[1])
    own_k.start()
    own_v.start()

    loads["w"].wait()
    for c in range(0, D, 256):
        w_t[c : c + 256, :] = w_f[:, c : c + 256].T.astype(jnp.bfloat16)
    dk_acc[...] = jnp.zeros_like(dk_acc)
    dv_acc[...] = jnp.zeros_like(dv_acc)
    gw[...] = jnp.zeros_like(gw)

    def pass_on(arrives, *then):
        ag_wait(arrives)
        for name in then:
            ag_send(name)

    def stage_b():
        pass_on("PB1", "P2B1", "XPB1")
        pass_on("MB2", "M2B2", "XMB2")
        pass_on("PB2", "XPB2")
        pass_on("MB1", "XMB1")

    def stage_x():
        pass_on("XA1", "PXA1", "MXA1")
        pass_on("XA2", "PXA2", "MXA2")

    def stage_a():
        pass_on("PA1", "P2A1")
        pass_on("MA2", "M2A2")

    def stage_2b():
        pass_on("P2B1", "XP2B1")
        pass_on("M2B2", "XM2B2")

    def stage_xa():
        pass_on("PXA1", "P2XA1")
        pass_on("MXA2", "M2XA2")

    def forward(p):
        q = qh[p * PAIR : (p + 1) * PAIR, :]
        s = nt(kh[...], q) * SCALE
        e = jnp.exp(s - jnp.max(s, axis=0, keepdims=True))
        prob = e / jnp.sum(e, axis=0, keepdims=True)
        att = nn(vt[...], prob.astype(jnp.bfloat16)).astype(jnp.bfloat16)
        for i in range(2):
            pt[2 * p + i] = prob[:, i * TOK : (i + 1) * TOK]
            at[2 * p + i] = att[:, i * TOK : (i + 1) * TOK]

    def span(first, count):
        return pl.ds(pl.multiple_of(first * TOK, TOK), count * TOK)

    def beside(ref, first, count):
        return jnp.concatenate([ref[first + i] for i in range(count)], axis=1)

    def pair_of(dy):
        return lax.rem(y + (dy + 8), 4) * 2

    def add_grad(first, count):
        gw[...] += nn(beside(at, first, count), do_all[span(first, count), :])

    def send_rows(j, st, out, dy):
        for dx in range(2):
            r = (dy % 4) * 2 + dx
            t = at_rel(dy, dx)
            if r:
                push(st.at[rows(t), :], out.at[:, cols(me)], back_s.at[j, r], back_r.at[j, r],
                     {"seq": t})

    def backward(first, count, last=False):
        here = span(first, count)
        q = qh[here, :]
        d_b = nn(do_all[here, :], w_t[...]).astype(jnp.bfloat16)
        d_t = d_b.astype(jnp.float32).T
        att = beside(at, first, count).astype(jnp.float32)
        row_dot = jnp.sum(d_t * att, axis=0, keepdims=True)
        prob = beside(pt, first, count)
        if last:
            dv_st[...] = (dv_acc[...] + nn(prob.astype(jnp.bfloat16), d_b)).astype(jnp.bfloat16)
            for away in (2, 1, -1, 0):
                send_rows(2, dv_st, dv_out, away)
        else:
            dv_acc[...] += nn(prob.astype(jnp.bfloat16), d_b)
        d_s = (prob * (nt(vh[...], d_b) - row_dot) * SCALE).astype(jnp.bfloat16)
        if last:
            dk_st[...] = (dk_acc[...] + nn(d_s, q)).astype(jnp.bfloat16)
            for away in (2, 1, -1, 0):
                send_rows(1, dk_st, dk_out, away)
        else:
            dk_acc[...] += nn(d_s, q)
        dq_st[here, :] = nn(kt[...], d_s).T.astype(jnp.bfloat16)
        if last:
            send_rows(0, dq_st, dq_out, 2)

    outs = ((dq_st, dq_out), (dk_st, dk_out), (dv_st, dv_out))

    stage_b()
    stage_x()

    @pl.when(ends)
    def _():
        pl.semaphore_signal(turn, inc=1, device_id={"agent": mate}, device_id_type=MESH)

    own_k.wait()
    own_v.wait()
    loads["q"].wait()
    a2a_wait(0, qh)
    a2a_wait(1, kh)
    a2a_wait(2, vh)
    kt[...] = kh[...].astype(jnp.float32).T.astype(jnp.bfloat16)
    vt[...] = vh[...].astype(jnp.float32).T.astype(jnp.bfloat16)
    forward(0)
    stage_a()
    forward(1)
    stage_2b()
    forward(2)
    stage_xa()
    forward(3)

    loads["d"].wait()
    loads["p"].wait()
    ps_f[...] = 2.0 * w_f[...] - ps_f[...]
    ag_wait("XB1", "XB2")
    add_grad(pair_of(0), 2)
    backward(pair_of(0), 2)
    send_rows(0, dq_st, dq_out, 0)

    ag_wait("PA2", "PXA2", "XPB1", "XPB2")
    add_grad(pair_of(-1), 2)
    backward(pair_of(-1), 2)
    send_rows(0, dq_st, dq_out, -1)

    ag_wait("MA1", "MXA1", "XMB1", "XMB2")
    add_grad(pair_of(1), 2)
    backward(pair_of(1), 2)
    send_rows(0, dq_st, dq_out, 1)

    ag_wait("P2A1", "M2A2")
    add_grad(at_rel(2, 0), 1)
    backward(at_rel(2, 0), 1)

    last = at_rel(2, 1)
    for n, (name, piece) in enumerate(LAST):
        ag_wait(name)
        first, width = PIECES[piece]
        for c in range(first, first + width, 128):
            g = gw[:, c : c + 128] + nn(at[last], do_all[rows(last), c : c + 128])
            gw[:, c : c + 128] = g
            phi = ps_f[:, c : c + 128] - 0.02 * g
            phi_f[:, c : c + 128] = phi
            phi_b[:, c : c + 128] = phi.astype(jnp.bfloat16)
        part = pl.ds(first, width)
        for i, other in enumerate((nxt, prv)):
            push(phi_b.at[:, part], halo.at[i, :, part], halo_s.at[i, n], halo_r.at[i, n],
                 {"agent": other})

    backward(last, 1, last=True)
    gw[...] = w_f[...] - 0.02 * gw[...]
    stores = [pltpu.make_async_copy(gw, np_out, out_sem.at[0])]
    stores[0].start()
    own = []
    for j, (st, out) in enumerate(outs):
        own.append(pltpu.make_async_copy(st.at[rows(me), :], out.at[:, cols(me)], own_sem.at[2 + j]))
        own[-1].start()

    loads["m"].wait()
    before = mix_ref[0, 0].astype(jnp.float32)
    after = mix_ref[0, 1].astype(jnp.float32)
    for n, (_, piece) in enumerate(LAST):
        first, width = PIECES[piece]
        part = pl.ds(first, width)
        for i in range(2):
            arrived(halo.at[i, :, part], halo_r.at[i, n], halo_s.at[i, n])
        c = slice(first, first + width)
        phi_f[:, c] = (
            (16.0 - before - after) * phi_f[:, c]
            + before * halo[0, :, c].astype(jnp.float32)
            + after * halo[1, :, c].astype(jnp.float32)
        ) * 0.0625
        stores.append(
            pltpu.make_async_copy(phi_f.at[:, part], nw_out.at[:, part], out_sem.at[1 + n])
        )
        stores[-1].start()
    for j, (st, out) in enumerate(outs):
        own[j].wait()
        for r, (dy, dx) in enumerate(rels):
            if r:
                arrived(out.at[:, cols(at_rel(-dy, dx))], back_r.at[j, r], back_s.at[j, r])
    for copy in stores:
        copy.wait()
    for copy in sent:
        copy.wait_send()


def store(*refs):
    ins, outs, held, load_sem, store_sem = refs[:5], refs[5:10], refs[10:15], refs[15], refs[16]
    loads, stores = [], []
    for i in range(5):
        loads.append(pltpu.make_async_copy(ins[i], held[i], load_sem.at[i]))
        stores.append(pltpu.make_async_copy(held[i], outs[i], store_sem.at[i]))
        loads[i].start()
    for load, copy in zip(loads, stores):
        load.wait()
        copy.start()
    for copy in stores:
        copy.wait()


def local(
    queries, key_codes, key_exps, value_codes, value_exps, d_out, out_weight, prev_psi, mixing
):
    bf, f32 = jnp.bfloat16, jnp.float32
    hbm = pl.BlockSpec(memory_space=pltpu.HBM)
    small, large = jax.ShapeDtypeStruct((TOK, HD), bf), jax.ShapeDtypeStruct((HDIM, D), f32)
    outs = pl.pallas_call(
        kernel,
        out_shape=[small] * 3 + [large] * 2,
        in_specs=[hbm] * 9,
        out_specs=[hbm] * 5,
        scratch_shapes=[
            pltpu.SMEM((1, 2), jnp.int32),
            pltpu.VMEM((1, HEADS), jnp.int32),
            pltpu.VMEM((1, HEADS), jnp.int32),
            pltpu.VMEM((TOK, HD), bf),
            pltpu.VMEM((TOK, HD), bf),
            pltpu.VMEM((TOK, HD), bf),
            pltpu.VMEM((TOK, HD), bf),
            pltpu.VMEM((TOKENS, HDIM), bf),
            pltpu.VMEM((TOKENS, HDIM), bf),
            pltpu.VMEM((TOKENS, HDIM), bf),
            pltpu.VMEM((HDIM, TOKENS), bf),
            pltpu.VMEM((HDIM, TOKENS), bf),
            pltpu.VMEM((TOKENS, D), bf),
            pltpu.VMEM((HDIM, D), f32),
            pltpu.VMEM((HDIM, D), f32),
            pltpu.VMEM((D, HDIM), bf),
            pltpu.VMEM((N_SEQ, TOKENS, TOK), f32),
            pltpu.VMEM((N_SEQ, HDIM, TOK), bf),
            pltpu.VMEM((HDIM, D), f32),
            pltpu.VMEM((TOKENS, HDIM), f32),
            pltpu.VMEM((TOKENS, HDIM), f32),
            pltpu.VMEM((TOKENS, HDIM), bf),
            pltpu.VMEM((TOKENS, HDIM), bf),
            pltpu.VMEM((TOKENS, HDIM), bf),
            pltpu.VMEM((HDIM, D), f32),
            pltpu.VMEM((HDIM, D), bf),
            pltpu.VMEM((2, HDIM, D), bf),
            pltpu.SemaphoreType.DMA((9,)),
            pltpu.SemaphoreType.DMA((5,)),
            pltpu.SemaphoreType.DMA((1 + len(LAST),)),
            pltpu.SemaphoreType.DMA((3, N_SEQ)),
            pltpu.SemaphoreType.DMA((3, N_SEQ)),
            pltpu.SemaphoreType.DMA((N_MSG,)),
            pltpu.SemaphoreType.DMA((N_MSG,)),
            pltpu.SemaphoreType.DMA((3, N_SEQ)),
            pltpu.SemaphoreType.DMA((3, N_SEQ)),
            pltpu.SemaphoreType.DMA((2, len(LAST))),
            pltpu.SemaphoreType.DMA((2, len(LAST))),
            pltpu.SemaphoreType.REGULAR,
        ],
        compiler_params=pltpu.CompilerParams(
            collective_id=0, has_side_effects=True, vmem_limit_bytes=VMEM
        ),
        cost_estimate=pl.CostEstimate(
            flops=2 * TOKENS * HDIM * (2 * D + 6 * TOKENS),
            bytes_accessed=8 * 1024 * 1024,
            transcendentals=TOKENS * TOKENS,
        ),
        name="exact_diffusion_step",
    )(
        mixing, key_exps[0], value_exps[0], queries[0], key_codes[0], value_codes[0],
        d_out[0], out_weight[0], prev_psi[0],
    )
    outs = pl.pallas_call(
        store,
        out_shape=[small] * 3 + [large] * 2,
        in_specs=[hbm] * 5,
        out_specs=[hbm] * 5,
        scratch_shapes=[pltpu.VMEM((TOK, HD), bf)] * 3
        + [pltpu.VMEM((HDIM, D), f32)] * 2
        + [pltpu.SemaphoreType.DMA((5,))] * 2,
        compiler_params=pltpu.CompilerParams(vmem_limit_bytes=VMEM),
        name="finish",
    )(*outs)
    return tuple(out[None] for out in outs)


def solution(mesh):
    rows = P("agent", "seq", None)
    return jax.shard_map(
        local,
        mesh=mesh,
        in_specs=(rows,) * 8 + (P("agent", None),),
        out_specs=(rows,) * 5,
        check_vma=False,
    )
```

```python
import jax
import jax.numpy as jnp
from jax import lax
from jax.experimental import pallas as pl
from jax.experimental.pallas import tpu as pltpu
from jax.sharding import PartitionSpec as P

HEADS = 8
HDIM = 128
TOK = 128
N_SEQ = 8
N_AGENT = 16
TOKENS = N_SEQ * TOK
HD = HEADS * HDIM
D = 2048
PAIR = 2 * TOK
VMEM = 62 * 1024 * 1024
SCALE = HDIM ** (-0.5)
MESH = pl.DeviceIdType.MESH

A1, A2, B1, B2 = (0, 640), (640, 640), (1280, 384), (1664, 384)
PIECES = {"A1": A1, "A2": A2, "B1": B1, "B2": B2}


def _gather_messages():
    msgs = []
    for p in ("B1", "B2", "A1", "A2"):
        msgs.append(("P" + p, "dn", (-1, 0), p))
        msgs.append(("M" + p, "up", (1, 0), p))
        msgs.append(("X" + p, "xp", (0, 1), p))
    for p in ("A1", "A2"):
        msgs.append(("PX" + p, "dn", (-1, 1), p))
        msgs.append(("MX" + p, "up", (1, 1), p))
    msgs.append(("P2A1", "dn", (-2, 0), "A1"))
    msgs.append(("P2XA1", "dn", (-2, 1), "A1"))
    msgs.append(("P2B1", "dn", (-2, 0), "B1"))
    msgs.append(("M2A2", "up", (2, 0), "A2"))
    msgs.append(("M2XA2", "up", (2, 1), "A2"))
    msgs.append(("M2B2", "up", (2, 0), "B2"))
    for p in ("B1", "B2"):
        msgs.append(("XP" + p, "xp", (-1, 1), p))
        msgs.append(("XM" + p, "xp", (1, 1), p))
    msgs.append(("XP2B1", "xp", (-2, 1), "B1"))
    msgs.append(("XM2B2", "xp", (2, 1), "B2"))
    return msgs


MSGS = _gather_messages()
KIND = {m[0]: i for i, m in enumerate(MSGS)}
N_MSG = len(MSGS)
LAST = (("XP2B1", "B1"), ("XM2B2", "B2"), ("P2XA1", "A1"), ("M2XA2", "A2"))


def nt(a, b):
    return lax.dot_general(a, b, (((1,), (1,)), ((), ())), preferred_element_type=jnp.float32)


def nn(a, b):
    return jnp.dot(a, b, preferred_element_type=jnp.float32)


def kernel(
    mix_hbm, ke_hbm, ve_hbm, q_hbm, kc_hbm, vc_hbm, do_hbm, w_hbm, ps_hbm,
    dq_out, dk_out, dv_out, nw_out, np_out,
    mix_ref, ke_ref, ve_ref, kc_v, vc_v, kv_st, qh, kvh, kt, vt, do_all, w_f, ps_f, w_t,
    pt, at, gw, dk_acc, dv_acc, dq_st, dk_st, dv_st, phi_f, phi_b, halo,
    load_sem, own_sem, out_sem, a2a_s, a2a_r, ag_s, ag_r, back_s, back_r, halo_s, halo_r, turn,
):
    me = lax.axis_index("seq")
    agent = lax.axis_index("agent")
    y, x = me // 2, lax.rem(me, 2)

    def at_rel(dy, dx):
        return lax.rem(y + (dy + 8), 4) * 2 + lax.rem(x + dx, 2)

    def rows(block):
        return pl.ds(pl.multiple_of(block * TOK, TOK), TOK)

    def cols(block):
        return pl.ds(pl.multiple_of(block * HDIM, HDIM), HDIM)

    rels = [(dy, dx) for dy in range(4) for dx in range(2)]
    peers = rels[1:]

    barrier = pltpu.get_barrier_semaphore()
    for dy, dx in peers:
        pl.semaphore_signal(barrier, inc=1, device_id={"seq": at_rel(dy, dx)}, device_id_type=MESH)
    nxt, prv = lax.rem(agent + 1, N_AGENT), lax.rem(agent + N_AGENT - 1, N_AGENT)
    for other in (nxt, prv):
        pl.semaphore_signal(barrier, inc=1, device_id={"agent": other}, device_id_type=MESH)
    loads = {}
    for i, (name, src, dst) in enumerate(
        (
            ("ke", ke_hbm, ke_ref),
            ("k", kc_hbm, kc_v),
            ("ve", ve_hbm, ve_ref),
            ("v", vc_hbm, vc_v),
            ("q", q_hbm.at[:, cols(me)], qh.at[rows(me), :]),
            ("w", w_hbm, w_f),
            ("d", do_hbm, do_all.at[rows(me), :]),
            ("p", ps_hbm, ps_f),
            ("m", mix_hbm, mix_ref),
        )
    ):
        loads[name] = pltpu.make_async_copy(src, dst, load_sem.at[i])
        loads[name].start()

    def scaled(codes, expo, out):
        factor = jnp.exp2(expo[...].astype(jnp.float32))
        for h in range(HEADS):
            c = slice(h * HDIM, (h + 1) * HDIM)
            kv_st[out, :, c] = (codes[:, c].astype(jnp.float32) * factor[0:1, h : h + 1]).astype(
                jnp.bfloat16
            )

    for codes, expo, out, a, b in (
        (kc_v, ke_ref, 0, "ke", "k"),
        (vc_v, ve_ref, 1, "ve", "v"),
    ):
        loads[a].wait()
        loads[b].wait()
        scaled(codes, expo, out)
    pl.semaphore_wait(barrier, len(peers) + 2)

    sent = []

    place = lax.rem(agent, 8)
    ends = jnp.logical_or(place == 0, place == 7)
    mates = jnp.logical_or(place == 1, place == 6)
    mate = agent + 1 - 2 * lax.rem(agent, 2)

    def push(src, dst, ssem, rsem, target):
        copy = pltpu.make_async_remote_copy(
            src_ref=src, dst_ref=dst, send_sem=ssem, recv_sem=rsem,
            device_id=target, device_id_type=MESH,
        )
        copy.start()
        sent.append(copy)

    def arrived(dst, rsem, ssem):
        pltpu.make_async_remote_copy(
            src_ref=dst, dst_ref=dst, send_sem=ssem, recv_sem=rsem,
            device_id={"seq": at_rel(0, 1)}, device_id_type=MESH,
        ).wait_recv()

    def rows_of(ref, block):
        return ref.at[rows(block), :] if len(ref.shape) == 2 else ref.at[:, rows(block), :]

    def a2a_send(j, src, dst):
        for r, (dy, dx) in enumerate(rels):
            if r:
                t = at_rel(dy, dx)
                push(src.at[..., cols(t)], rows_of(dst, me), a2a_s.at[j, r], a2a_r.at[j, r], {"seq": t})

    def a2a_wait(j, dst):
        for r, (dy, dx) in enumerate(rels):
            if r:
                arrived(rows_of(dst, at_rel(-dy, dx)), a2a_r.at[j, r], a2a_s.at[j, r])

    a2a_send(0, q_hbm, qh)
    a2a_send(1, kv_st, kvh)

    step = {"xp": (0, 1), "up": (1, 0), "dn": (-1, 0)}
    back_to = {"xp": "xp", "up": "dn", "dn": "up"}

    def ag_send(name, own=False):
        kind = KIND[name]
        _, source, (dy, dx), piece = MSGS[kind]
        sy, sx = step[source]
        ty, tx = step[back_to[source]]
        block = at_rel(dy - sy, (dx + sx) % 2)
        first, width = PIECES[piece]
        here = do_all.at[rows(block), pl.ds(first, width)]
        src = do_hbm.at[:, pl.ds(first, width)] if own else here
        push(src, here, ag_s.at[kind], ag_r.at[kind], {"seq": at_rel(ty, tx)})

    def ag_wait(*names):
        for name in names:
            kind = KIND[name]
            _, _, (dy, dx), piece = MSGS[kind]
            first, width = PIECES[piece]
            here = do_all.at[rows(at_rel(dy, dx)), pl.ds(first, width)]
            arrived(here, ag_r.at[kind], ag_s.at[kind])

    @pl.when(mates)
    def _():
        pl.semaphore_wait(turn, 1)

    for name in ("PB1", "MB2", "XA1", "PB2", "MB1", "XA2", "PA1", "MA2", "PA2", "MA1", "XB1", "XB2"):
        ag_send(name, own=True)

    own_kv = pltpu.make_async_copy(kv_st.at[:, :, cols(me)], kvh.at[:, rows(me), :], own_sem.at[0])
    own_kv.start()

    loads["w"].wait()
    for c in range(0, D, 256):
        w_t[c : c + 256, :] = w_f[:, c : c + 256].T.astype(jnp.bfloat16)
    dk_acc[...] = jnp.zeros_like(dk_acc)
    dv_acc[...] = jnp.zeros_like(dv_acc)
    gw[...] = jnp.zeros_like(gw)

    def pass_on(arrives, *then):
        ag_wait(arrives)
        for name in then:
            ag_send(name)

    def stage_b():
        pass_on("PB1", "P2B1", "XPB1")
        pass_on("MB2", "M2B2", "XMB2")
        pass_on("PB2", "XPB2")
        pass_on("MB1", "XMB1")

    def stage_x():
        pass_on("XA1", "PXA1", "MXA1")
        pass_on("XA2", "PXA2", "MXA2")

    def stage_a():
        pass_on("PA1", "P2A1")
        pass_on("MA2", "M2A2")

    def stage_2b():
        pass_on("P2B1", "XP2B1")
        pass_on("M2B2", "XM2B2")

    def stage_xa():
        pass_on("PXA1", "P2XA1")
        pass_on("MXA2", "M2XA2")

    def forward(p):
        q = qh[p * PAIR : (p + 1) * PAIR, :]
        s = nt(kvh[0], q) * SCALE
        e = jnp.exp(s - jnp.max(s, axis=0, keepdims=True))
        prob = e / jnp.sum(e, axis=0, keepdims=True)
        att = nn(vt[...], prob.astype(jnp.bfloat16)).astype(jnp.bfloat16)
        for i in range(2):
            pt[2 * p + i] = prob[:, i * TOK : (i + 1) * TOK]
            at[2 * p + i] = att[:, i * TOK : (i + 1) * TOK]

    def span(first, count):
        return pl.ds(pl.multiple_of(first * TOK, TOK), count * TOK)

    def beside(ref, first, count):
        return jnp.concatenate([ref[first + i] for i in range(count)], axis=1)

    def pair_of(dy):
        return lax.rem(y + (dy + 8), 4) * 2

    def add_grad(first, count):
        gw[...] += nn(beside(at, first, count), do_all[span(first, count), :])

    def send_rows(j, st, out, dy):
        for dx in range(2):
            r = (dy % 4) * 2 + dx
            t = at_rel(dy, dx)
            if r:
                push(st.at[rows(t), :], out.at[:, cols(me)], back_s.at[j, r], back_r.at[j, r],
                     {"seq": t})

    def backward(first, count, last=False):
        here = span(first, count)
        q = qh[here, :]
        d_b = nn(do_all[here, :], w_t[...]).astype(jnp.bfloat16)
        d_t = d_b.astype(jnp.float32).T
        att = beside(at, first, count).astype(jnp.float32)
        row_dot = jnp.sum(d_t * att, axis=0, keepdims=True)
        prob = beside(pt, first, count)
        if last:
            dv_st[...] = (dv_acc[...] + nn(prob.astype(jnp.bfloat16), d_b)).astype(jnp.bfloat16)
            for away in (2, 1, -1, 0):
                send_rows(2, dv_st, dv_out, away)
        else:
            dv_acc[...] += nn(prob.astype(jnp.bfloat16), d_b)
        d_s = (prob * (nt(kvh[1], d_b) - row_dot) * SCALE).astype(jnp.bfloat16)
        if last:
            dk_st[...] = (dk_acc[...] + nn(d_s, q)).astype(jnp.bfloat16)
            for away in (2, 1, -1, 0):
                send_rows(1, dk_st, dk_out, away)
        else:
            dk_acc[...] += nn(d_s, q)
        dq_st[here, :] = nn(kt[...], d_s).T.astype(jnp.bfloat16)
        if last:
            send_rows(0, dq_st, dq_out, 2)

    outs = ((dq_st, dq_out), (dk_st, dk_out), (dv_st, dv_out))

    stage_b()
    stage_x()

    @pl.when(ends)
    def _():
        pl.semaphore_signal(turn, inc=1, device_id={"agent": mate}, device_id_type=MESH)

    own_kv.wait()
    loads["q"].wait()
    a2a_wait(0, qh)
    a2a_wait(1, kvh)
    kt[...] = kvh[0].astype(jnp.float32).T.astype(jnp.bfloat16)
    vt[...] = kvh[1].astype(jnp.float32).T.astype(jnp.bfloat16)
    forward(0)
    stage_a()
    forward(1)
    stage_2b()
    forward(2)
    stage_xa()
    forward(3)

    loads["d"].wait()
    loads["p"].wait()
    ps_f[...] = 2.0 * w_f[...] - ps_f[...]
    ag_wait("XB1", "XB2")
    add_grad(pair_of(0), 2)
    backward(pair_of(0), 2)
    send_rows(0, dq_st, dq_out, 0)

    ag_wait("PA2", "PXA2", "XPB1", "XPB2")
    add_grad(pair_of(-1), 2)
    backward(pair_of(-1), 2)
    send_rows(0, dq_st, dq_out, -1)

    ag_wait("MA1", "MXA1", "XMB1", "XMB2")
    add_grad(pair_of(1), 2)
    backward(pair_of(1), 2)
    send_rows(0, dq_st, dq_out, 1)

    ag_wait("P2A1", "M2A2")
    add_grad(at_rel(2, 0), 1)
    backward(at_rel(2, 0), 1)

    last = at_rel(2, 1)
    for n, (name, piece) in enumerate(LAST):
        ag_wait(name)
        first, width = PIECES[piece]
        for c in range(first, first + width, 128):
            g = gw[:, c : c + 128] + nn(at[last], do_all[rows(last), c : c + 128])
            gw[:, c : c + 128] = g
            phi = ps_f[:, c : c + 128] - 0.02 * g
            phi_f[:, c : c + 128] = phi
            phi_b[:, c : c + 128] = phi.astype(jnp.bfloat16)
        part = pl.ds(first, width)
        for i, other in enumerate((nxt, prv)):
            push(phi_b.at[:, part], halo.at[i, :, part], halo_s.at[i, n], halo_r.at[i, n],
                 {"agent": other})

    early, sent[:] = sent[:], []
    backward(last, 1, last=True)
    gw[...] = w_f[...] - 0.02 * gw[...]
    stores = [pltpu.make_async_copy(gw, np_out, out_sem.at[0])]
    stores[0].start()
    while early:
        early.pop().wait_send()
    own = []
    for j, (st, out) in enumerate(outs):
        own.append(pltpu.make_async_copy(st.at[rows(me), :], out.at[:, cols(me)], own_sem.at[2 + j]))
        own[-1].start()

    loads["m"].wait()
    before = mix_ref[0, 0].astype(jnp.float32)
    after = mix_ref[0, 1].astype(jnp.float32)
    for n, (_, piece) in enumerate(LAST):
        first, width = PIECES[piece]
        part = pl.ds(first, width)
        for i in range(2):
            arrived(halo.at[i, :, part], halo_r.at[i, n], halo_s.at[i, n])
        c = slice(first, first + width)
        phi_f[:, c] = (
            (16.0 - before - after) * phi_f[:, c]
            + before * halo[0, :, c].astype(jnp.float32)
            + after * halo[1, :, c].astype(jnp.float32)
        ) * 0.0625
        stores.append(
            pltpu.make_async_copy(phi_f.at[:, part], nw_out.at[:, part], out_sem.at[1 + n])
        )
        stores[-1].start()
    for j in (0, 2, 1):
        _, out = outs[j]
        own[j].wait()
        for r, (dy, dx) in enumerate(rels):
            if r:
                arrived(out.at[:, cols(at_rel(-dy, dx))], back_r.at[j, r], back_s.at[j, r])
    for copy in stores:
        copy.wait()
    for copy in sent:
        copy.wait_send()


def store(*refs):
    ins, outs, held, load_sem, store_sem = refs[:5], refs[5:10], refs[10:15], refs[15], refs[16]
    loads, stores = [], []
    for i in range(5):
        loads.append(pltpu.make_async_copy(ins[i], held[i], load_sem.at[i]))
        stores.append(pltpu.make_async_copy(held[i], outs[i], store_sem.at[i]))
        loads[i].start()
    for load, copy in zip(loads, stores):
        load.wait()
        copy.start()
    for copy in stores:
        copy.wait()


def local(
    queries, key_codes, key_exps, value_codes, value_exps, d_out, out_weight, prev_psi, mixing
):
    bf, f32 = jnp.bfloat16, jnp.float32
    hbm = pl.BlockSpec(memory_space=pltpu.HBM)
    small, large = jax.ShapeDtypeStruct((TOK, HD), bf), jax.ShapeDtypeStruct((HDIM, D), f32)
    outs = pl.pallas_call(
        kernel,
        out_shape=[small] * 3 + [large] * 2,
        in_specs=[hbm] * 9,
        out_specs=[hbm] * 5,
        scratch_shapes=[
            pltpu.SMEM((1, 2), jnp.int32),
            pltpu.VMEM((1, HEADS), jnp.int32),
            pltpu.VMEM((1, HEADS), jnp.int32),
            pltpu.VMEM((TOK, HD), bf),
            pltpu.VMEM((TOK, HD), bf),
            pltpu.VMEM((2, TOK, HD), bf),
            pltpu.VMEM((TOKENS, HDIM), bf),
            pltpu.VMEM((2, TOKENS, HDIM), bf),
            pltpu.VMEM((HDIM, TOKENS), bf),
            pltpu.VMEM((HDIM, TOKENS), bf),
            pltpu.VMEM((TOKENS, D), bf),
            pltpu.VMEM((HDIM, D), f32),
            pltpu.VMEM((HDIM, D), f32),
            pltpu.VMEM((D, HDIM), bf),
            pltpu.VMEM((N_SEQ, TOKENS, TOK), f32),
            pltpu.VMEM((N_SEQ, HDIM, TOK), bf),
            pltpu.VMEM((HDIM, D), f32),
            pltpu.VMEM((TOKENS, HDIM), f32),
            pltpu.VMEM((TOKENS, HDIM), f32),
            pltpu.VMEM((TOKENS, HDIM), bf),
            pltpu.VMEM((TOKENS, HDIM), bf),
            pltpu.VMEM((TOKENS, HDIM), bf),
            pltpu.VMEM((HDIM, D), f32),
            pltpu.VMEM((HDIM, D), bf),
            pltpu.VMEM((2, HDIM, D), bf),
            pltpu.SemaphoreType.DMA((9,)),
            pltpu.SemaphoreType.DMA((5,)),
            pltpu.SemaphoreType.DMA((1 + len(LAST),)),
            pltpu.SemaphoreType.DMA((3, N_SEQ)),
            pltpu.SemaphoreType.DMA((3, N_SEQ)),
            pltpu.SemaphoreType.DMA((N_MSG,)),
            pltpu.SemaphoreType.DMA((N_MSG,)),
            pltpu.SemaphoreType.DMA((3, N_SEQ)),
            pltpu.SemaphoreType.DMA((3, N_SEQ)),
            pltpu.SemaphoreType.DMA((2, len(LAST))),
            pltpu.SemaphoreType.DMA((2, len(LAST))),
            pltpu.SemaphoreType.REGULAR,
        ],
        compiler_params=pltpu.CompilerParams(
            collective_id=0, has_side_effects=True, vmem_limit_bytes=VMEM
        ),
        cost_estimate=pl.CostEstimate(
            flops=2 * TOKENS * HDIM * (2 * D + 6 * TOKENS),
            bytes_accessed=8 * 1024 * 1024,
            transcendentals=TOKENS * TOKENS,
        ),
        name="exact_diffusion_step",
    )(
        mixing, key_exps[0], value_exps[0], queries[0], key_codes[0], value_codes[0],
        d_out[0], out_weight[0], prev_psi[0],
    )
    outs = pl.pallas_call(
        store,
        out_shape=[small] * 3 + [large] * 2,
        in_specs=[hbm] * 5,
        out_specs=[hbm] * 5,
        scratch_shapes=[pltpu.VMEM((TOK, HD), bf)] * 3
        + [pltpu.VMEM((HDIM, D), f32)] * 2
        + [pltpu.SemaphoreType.DMA((5,))] * 2,
        compiler_params=pltpu.CompilerParams(vmem_limit_bytes=VMEM),
        name="finish",
    )(*outs)
    return tuple(out[None] for out in outs)


def solution(mesh):
    rows = P("agent", "seq", None)
    return jax.shard_map(
        local,
        mesh=mesh,
        in_specs=(rows,) * 8 + (P("agent", None),),
        out_specs=(rows,) * 5,
        check_vma=False,
    )
```
